32 devices in a mesh: clip: 8 (over y, x, core), seq: 4 (over z).
Axes of the slice: x: 2, y: 2, z: 4, core: 2. Of those that a mesh axis runs over, the one named last changes fastest.
Arguments:
- frames: bfloat16 [8, 4, 16, 16, 320], P('clip', 'seq'), may hold values from -6 to 6
- cotangent: bfloat16 [8, 4, 16, 16, 320], P('clip', 'seq'), may hold values from -6 to 6
- w_space: bfloat16 [320, 9, 320], P('seq'), may hold values from -0.109375 to 0.109375
- w_time: bfloat16 [3, 320, 320], replicated, may hold values from -0.1875 to 0.1875
Outputs:
- frames_grad: bfloat16 [8, 4, 16, 16, 320], P('clip', 'seq')
- space_grad: float32 [320, 9, 320], P('seq')
- time_grad: float32 [3, 320, 320], replicated
The draws below stay inside these ranges and needn't reach their ends.
All inputs are finite; a program needn't handle non-finite values.
Results may differ from the reference program's by a relative error of at most 0.0085.
Values may be sent and summed in bfloat16 or wider, within the bound.
No kernel may reach another device: no remote copies, remote signals or barrier semaphores. Data moves between devices by JAX's collectives and lax.ppermute only.
A program may use at most 64 MiB of HBM per device.

```python
import math
import jax
import jax.numpy as jnp
from jax import lax

C = 320
H = 16
W = 16
FRAMES = 4
CLIPS = 8


def spiked(entries, key, source, target, parts, factor):
    owner, partner = [(jnp.arange(entries.shape[dim]) // (entries.shape[dim] // parts)).reshape([-1 if axis == dim else 1 for axis in range(entries.ndim)]) for dim in (source, target)]
    chosen = jax.random.permutation(key, parts)[partner]
    strong = (owner == chosen) | (owner == (partner + parts // 2) % parts)
    return jnp.where(strong, factor * entries, entries)


def block_scale(key, shape, cuts, smallest, high):
    def one(position, shards_of):
        steps = jax.random.uniform(jax.random.fold_in(jax.random.fold_in(key, 6), position), (shards_of,), jnp.float32, smallest / len(cuts), high / len(cuts))
        return jnp.repeat(jnp.exp(steps), shape[position] // shards_of).reshape((-1,) + (1,) * (len(shape) - position - 1))

    loudness = one(*cuts[0])
    for cut in cuts[1:]:
        loudness = loudness * one(*cut)
    return loudness


def centred(key, extent, spread, bound, cuts=(), dtype=jnp.bfloat16):
    result = spread * jax.random.normal(key, extent, jnp.float32)
    if cuts:
        result = result * block_scale(key, extent, cuts, -0.22, 0.18)
    return jnp.clip(result, -bound, bound).astype(dtype)


def gaussian_with(own_key, dims, scale, limit, cuts, heavy, held_as=jnp.bfloat16):
    values = scale * jax.random.normal(own_key, dims, jnp.float32)
    if cuts:
        values = values * block_scale(own_key, dims, cuts, -0.22, 0.18)
    return jnp.clip(spiked(values, jax.random.fold_in(own_key, 3), *heavy), -limit, limit).astype(held_as)


def setup_inputs(seed: int = 0) -> dict:
    seeds = jax.random.split(jax.random.key(seed), 5)
    return {
        "frames": gaussian_with(seeds[0], (CLIPS, FRAMES, H, W, C), 1.0, 6.0, ((0, 8), (1, 4)), (1, 4, 4, 2.0)),
        "cotangent": centred(seeds[1], (CLIPS, FRAMES, H, W, C), 1.0, 6.0, ((0, 8), (1, 4))),
        "w_space": centred(seeds[2], (C, 9, C), (9 * C) ** -0.5, 0.109375, ((0, 4),)),
        "w_time": centred(seeds[3], (3, C, C), (3 * C) ** -0.5, 0.1875),
    }


def clip_grads(clip_x, clip_g, w_space, w_time):
    count, height, width, chans = clip_x.shape
    padded = jnp.pad(clip_x, ((0, 0), (1, 1), (1, 1), (0, 0)))
    pieces = [padded[:, i:i + height, j:j + width, :].reshape(-1, chans) for i in range(3) for j in range(3)]
    pre_act = jnp.zeros((count * height * width, chans), jnp.float32)
    for tap in range(9):
        pre_act = pre_act + jnp.dot(pieces[tap], w_space[:, tap, :], preferred_element_type=jnp.float32)
    acts = jax.nn.silu(pre_act).astype(jnp.bfloat16)
    g_flat = clip_g.reshape(count, height * width, chans)
    g_pad = jnp.pad(g_flat, ((1, 1), (0, 0), (0, 0)))
    act_grad = jnp.zeros((count * height * width, chans), jnp.float32)
    time_terms = []
    for k in range(3):
        shifted = g_pad[2 - k:2 - k + count].reshape(-1, chans)
        act_grad = act_grad + jnp.dot(shifted, w_time[k].T, preferred_element_type=jnp.float32)
        time_terms.append(jnp.dot(acts.T, shifted, preferred_element_type=jnp.float32))
    act_grad = act_grad.astype(jnp.bfloat16)
    sigma = jax.nn.sigmoid(pre_act)
    pre_grad = (act_grad.astype(jnp.float32) * sigma * (1.0 + pre_act * (1.0 - sigma))).astype(jnp.bfloat16)
    space_terms = jnp.stack([jnp.dot(pieces[tap].T, pre_grad, preferred_element_type=jnp.float32) for tap in range(9)], axis=1)
    grad_pad = jnp.pad(pre_grad.reshape(count, height, width, chans), ((0, 0), (1, 1), (1, 1), (0, 0)))
    input_grad = clip_g.reshape(-1, chans).astype(jnp.float32)
    for i in range(3):
        for j in range(3):
            piece = grad_pad[:, 2 - i:2 - i + height, 2 - j:2 - j + width, :].reshape(-1, chans)
            input_grad = input_grad + jnp.dot(piece, w_space[:, 3 * i + j, :].T, preferred_element_type=jnp.float32)
    input_grad = input_grad.astype(jnp.bfloat16).reshape(count, height, width, chans)
    return (input_grad, space_terms, jnp.stack(time_terms, axis=0))

def reference(frames, cotangent, w_space, w_time):
    clips, count, height, width, chans = frames.shape
    factor = 1.0 / math.sqrt(clips * count * height * width)

    def one_clip(carry, pair):
        space_acc, time_acc = carry
        input_grad, space_terms, time_terms = clip_grads(pair[0], pair[1], w_space, w_time)
        return ((space_acc + space_terms, time_acc + time_terms), input_grad)
    start = (jnp.zeros((chans, 9, chans), jnp.float32), jnp.zeros((3, chans, chans), jnp.float32))
    (space_acc, time_acc), frames_grad = lax.scan(one_clip, start, (frames, cotangent))
    return (frames_grad, space_acc * factor, time_acc * factor)
```

```python
import functools
import math

import jax
import jax.numpy as jnp
from jax import lax
from jax.experimental import pallas as pl
from jax.experimental.pallas import tpu as pltpu
from jax.sharding import PartitionSpec as P


def padded_2(cells, sides, width):
    for axis, dim in sides:
        count = lax.axis_size(axis)
        ends = count - 1
        head = lax.slice_in_dim(cells, 0, width, axis=dim)
        tail = lax.slice_in_dim(cells, cells.shape[dim] - width, cells.shape[dim], axis=dim)
        cells = jnp.concatenate(
            [
                lax.ppermute(tail, axis, [(i, (i + 1) % count) for i in range(ends)]),
                cells,
                lax.ppermute(head, axis, [((i + 1) % count, i) for i in range(ends)]),
            ],
            axis=dim,
        )
    return cells


def temporal_grads(acts, g_pad, w_time):
    count = acts.shape[0]
    chans = acts.shape[-1]
    flat_acts = acts.reshape(-1, chans)
    act_grad = jnp.zeros(flat_acts.shape, jnp.float32)
    time_terms = []
    for k in range(3):
        shifted = g_pad[2 - k : 2 - k + count].reshape(-1, chans)
        act_grad = act_grad + lax.dot_general(
            shifted, w_time[k], (((1,), (1,)), ((), ())), preferred_element_type=jnp.float32
        )
        time_terms.append(
            lax.dot_general(
                flat_acts, shifted, (((0,), (0,)), ((), ())), preferred_element_type=jnp.float32
            )
        )
    return (act_grad.astype(jnp.bfloat16).reshape(acts.shape), jnp.stack(time_terms, axis=0))


def per_device_general(frames, cotangent, w_space, w_time):
    weights = lax.all_gather(w_space, "seq", axis=0, tiled=True)
    clip_x = frames[0]
    clip_g = cotangent[0]
    count, height, width, chans = clip_x.shape
    factor = 1.0 / math.sqrt(lax.axis_size("clip") * count * lax.axis_size("seq") * height * width)
    padded = jnp.pad(clip_x, ((0, 0), (1, 1), (1, 1), (0, 0)))
    pieces = [
        padded[:, i : i + height, j : j + width, :].reshape(-1, chans)
        for i in range(3)
        for j in range(3)
    ]
    pre_act = jnp.zeros((count * height * width, chans), jnp.float32)
    for tap in range(9):
        pre_act = pre_act + jnp.dot(
            pieces[tap], weights[:, tap, :], preferred_element_type=jnp.float32
        )
    acts = jax.nn.silu(pre_act).astype(jnp.bfloat16).reshape(1, count, height, width, chans)
    g_rims = padded_2(cotangent, (("seq", 1),), 1)
    g_pad = g_rims[0].reshape(count + 2, height * width, chans)
    act_grad, time_terms = temporal_grads(
        acts[0].reshape(count, height * width, chans), g_pad, w_time
    )
    sigma = jax.nn.sigmoid(pre_act)
    pre_grad = (
        act_grad.reshape(-1, chans).astype(jnp.float32) * sigma * (1.0 + pre_act * (1.0 - sigma))
    ).astype(jnp.bfloat16)
    terms = []
    for tap in range(9):
        part = pieces[tap]
        terms.append(
            lax.dot_general(
                part, pre_grad, (((0,), (0,)), ((), ())), preferred_element_type=jnp.float32
            )
        )
    space_share = lax.psum_scatter(
        jnp.stack(terms, axis=1) * factor, "seq", scatter_dimension=0, tiled=True
    )
    space_grad = lax.psum(space_share, "clip")
    time_grad = lax.psum(time_terms * factor, ("clip", "seq"))
    grad_pad = jnp.pad(
        pre_grad.reshape(count, height, width, chans), ((0, 0), (1, 1), (1, 1), (0, 0))
    )
    input_grad = clip_g.reshape(-1, chans).astype(jnp.float32)
    for i in range(3):
        for j in range(3):
            piece = grad_pad[:, 2 - i : 2 - i + height, 2 - j : 2 - j + width, :].reshape(-1, chans)
            input_grad = input_grad + lax.dot_general(
                piece,
                weights[:, 3 * i + j, :],
                (((1,), (1,)), ((), ())),
                preferred_element_type=jnp.float32,
            )
    frames_grad = input_grad.astype(jnp.bfloat16).reshape(1, count, height, width, chans)
    return (frames_grad, space_grad, time_grad)


BF16 = jnp.bfloat16
F32 = jnp.float32
LANES = 128
VMEM = pl.BlockSpec(memory_space=pltpu.VMEM)
NN = (((1,), (0,)), ((), ()))
NT = (((1,), (1,)), ((), ()))
TN = (((0,), (0,)), ((), ()))


def round_up(value, unit):
    return -(-value // unit) * unit


def mm(lhs, rhs, dims):
    return lax.dot_general(lhs, rhs, dims, preferred_element_type=F32)


def call(kernel, outs, *args, scratch=()):
    return pl.pallas_call(
        kernel,
        out_shape=tuple(jax.ShapeDtypeStruct(shape, dtype) for shape, dtype in outs),
        in_specs=[VMEM] * len(args),
        out_specs=(VMEM,) * len(outs),
        scratch_shapes=list(scratch),
        compiler_params=pltpu.CompilerParams(vmem_limit_bytes=48 * 1024 * 1024),
    )(*args)


class Plan:
    def __init__(self, clips, seqs, height, width, chans):
        self.clips, self.seqs = clips, seqs
        self.height, self.width, self.chans = height, width, chans
        self.group = clips // 2
        self.slab = chans // max(self.group, 1)
        self.rows = chans // seqs
        self.pixels = height * width
        self.cols = 9 * self.slab
        self.half = round_up(round_up(self.cols, 2 * LANES) // 2, LANES)
        self.tcols = round_up(3 * self.slab, LANES)
        self.thalf = chans // 2
        self.factor = 1.0 / math.sqrt(clips * seqs * self.pixels)

    def fits(self):
        return (
            self.group == 4
            and self.slab * self.group == self.chans
            and self.rows * self.seqs == self.chans
            and self.slab % 16 == 0
            and self.rows % 16 == 0
            and self.thalf % 16 == 0
            and self.pixels % LANES == 0
            and self.seqs >= 2
        )

    def place(self):
        clip = lax.axis_index("clip")
        return clip % self.group, clip // self.group, lax.axis_index("seq")


def prepare(plan, f_ref, g_ref, w_ref, fg_ref, gt_ref, wp_ref):
    low, _, _ = plan.place()
    chans, slab = plan.chans, plan.slab
    grad = g_ref[...].T
    gt_ref[...] = grad
    fg_ref[chans:, :] = grad
    fg_ref[:chans, :] = f_ref[...].T
    for index in range(plan.group):

        @pl.when(low == index)
        def _():
            wp_ref[...] = jnp.concatenate(
                [w_ref[tap][:, slab * index : slab * (index + 1)] for tap in range(9)], axis=1
            )


def shifts(plan, lanes):
    lane = lax.broadcasted_iota(jnp.int32, (1, lanes), 1) % plan.pixels
    row, col = lane // plan.width, lane % plan.width
    found = []
    for i in range(3):
        for j in range(3):
            inside = (
                (row + (i - 1) >= 0)
                & (row + (i - 1) < plan.height)
                & (col + (j - 1) >= 0)
                & (col + (j - 1) < plan.width)
            )
            found.append(((i - 1) * plan.width + (j - 1), inside))
    return found


def rolled(value, distance):
    lanes = value.shape[1]
    return value if distance == 0 else pltpu.roll(value, (-distance) % lanes, 1)


def group_frames(plan, own_ref, pair_ref, core_ref, part):
    chans = plan.chans
    first = slice(part * chans, (part + 1) * chans)
    second = slice((2 + part) * chans, (3 + part) * chans)
    return [own_ref[first, :], core_ref[first, :], pair_ref[first, :], core_ref[second, :]]


def forward(plan, *refs):
    w_refs = refs[: plan.seqs]
    own_ref, pair_ref, core_ref = refs[plan.seqs : plan.seqs + 3]
    w_all, f_all, a_ref, d_ref = refs[plan.seqs + 3 : plan.seqs + 7]
    taps = refs[plan.seqs + 7]
    _, _, z = plan.place()
    rows, slab = plan.rows, plan.slab
    for k, w_ref in enumerate(w_refs):
        owner = (z - k + plan.seqs) % plan.seqs
        w_all[pl.ds(pl.multiple_of(owner * rows, 16), rows), :] = w_ref[...]
    for d, frame in enumerate(group_frames(plan, own_ref, pair_ref, core_ref, 0)):
        f_all[:, d * plan.pixels : (d + 1) * plan.pixels] = frame
    taps[...] = mm(w_all[...], f_all[...], TN)
    total = None
    for tap, (distance, inside) in enumerate(shifts(plan, f_all.shape[1])):
        term = rolled(taps[tap * slab : (tap + 1) * slab, :], distance)
        term = jnp.where(inside, term, 0.0)
        total = term if total is None else total + term
    sigma = 1.0 / (1.0 + jnp.exp(-total))
    a_ref[...] = (total * sigma).astype(BF16)
    d_ref[...] = sigma * (1.0 + total * (1.0 - sigma))


def cotangents(plan, fg_refs, halo_refs):
    before = group_frames(plan, *halo_refs, 0)
    after = group_frames(plan, *halo_refs, 1)
    here = group_frames(plan, *fg_refs, 1)
    return [after, here, before]


def temporal(plan, a_ref, *refs):
    fg_refs, halo_refs = refs[:3], refs[3:6]
    send_ref, keep_ref, total = refs[6:]
    _, high, _ = plan.place()
    pixels = plan.pixels
    acts = a_ref[...]
    parts = []
    for grads in cotangents(plan, fg_refs, halo_refs):
        term = None
        for d, grad in enumerate(grads):
            here = mm(grad, acts[:, d * pixels : (d + 1) * pixels], NT)
            term = here if term is None else term + here
        parts.append(term)
    pad = plan.tcols - 3 * plan.slab
    if pad:
        parts.append(jnp.zeros((plan.chans, pad), F32))
    total[...] = jnp.concatenate(parts, axis=1)
    size = plan.thalf
    keep_ref[...] = total[pl.ds(pl.multiple_of(high * size, 16), size), :]
    send_ref[...] = total[pl.ds(pl.multiple_of((1 - high) * size, 16), size), :].astype(BF16)


def spatial(plan, *refs):
    w_all, f_all, d_ref, wt_ref = refs[:4]
    fg_refs, halo_refs = refs[4:7], refs[7:10]
    s_send, s_keep, f_send, f_keep, expanded, total = refs[10:]
    low, high, _ = plan.place()
    pixels, slab, chans = plan.pixels, plan.slab, plan.chans
    parts = [None] * plan.group
    for k, grads in enumerate(cotangents(plan, fg_refs, halo_refs)):
        weight = wt_ref[k, pl.ds(pl.multiple_of(low * slab, 16), slab), :]
        for d, grad in enumerate(grads):
            here = mm(weight, grad, NN)
            parts[d] = here if parts[d] is None else parts[d] + here
    act_grad = jnp.concatenate(parts, axis=1).astype(BF16).astype(F32)
    pre_grad = (act_grad * d_ref[...]).astype(BF16).astype(F32)
    for tap, (distance, _) in enumerate(shifts(plan, pre_grad.shape[1])):
        inside = shifts(plan, pre_grad.shape[1])[8 - tap][1]
        term = jnp.where(inside, rolled(pre_grad, -distance), 0.0)
        expanded[tap * slab : (tap + 1) * slab, :] = term.astype(BF16)
    total[:, : plan.cols] = mm(f_all[...], expanded[...], NT)
    if plan.cols < total.shape[1]:
        total[:, plan.cols :] = jnp.zeros((chans, total.shape[1] - plan.cols), F32)
    size = plan.half
    s_keep[...] = total[:, pl.ds(pl.multiple_of(high * size, LANES), size)]
    s_send[...] = total[:, pl.ds(pl.multiple_of((1 - high) * size, LANES), size)].astype(BF16)
    grads = mm(w_all[...], expanded[...], NN)
    for d in range(2):
        f_keep[d * chans : (d + 1) * chans, :] = grads[:, d * pixels : (d + 1) * pixels]
        there = grads[:, (2 + d) * pixels : (3 + d) * pixels]
        f_send[d * chans : (d + 1) * chans, :] = there.astype(BF16)


def frame_half(plan, keep_ref, got_ref, send_ref, own_ref):
    chans = plan.chans
    own_ref[...] = keep_ref[:chans, :] + got_ref[:chans, :].astype(F32)
    send_ref[...] = (keep_ref[chans:, :] + got_ref[chans:, :].astype(F32)).astype(BF16)


def frame_end(plan, own_ref, got_ref, g_ref, out_ref):
    total = own_ref[...] + got_ref[...].astype(F32)
    out_ref[...] = (g_ref[...].astype(F32) + total.T).astype(BF16)


def space_rows(plan, keep_ref, got_ref, *refs):
    own_ref, send_refs, total = refs[0], refs[1:-1], refs[-1]
    _, _, z = plan.place()
    total[...] = keep_ref[...] + got_ref[...].astype(F32)
    rows = plan.rows
    own_ref[...] = total[pl.ds(pl.multiple_of(z * rows, 16), rows), :]
    for k, ref in enumerate(send_refs, 1):
        other = (z + k) % plan.seqs
        ref[...] = total[pl.ds(pl.multiple_of(other * rows, 16), rows), :].astype(BF16)


def space_end(plan, *refs):
    pieces, out_ref, held = refs[:-2], refs[-2], refs[-1]
    low, high, _ = plan.place()
    group, slab = plan.group, plan.slab
    for m, piece in enumerate(pieces):
        other = high if m < group else 1 - high
        lane = pl.multiple_of(other * plan.half, LANES)
        held[low ^ (m % group), :, pl.ds(lane, plan.half)] = piece[...].astype(F32) * plan.factor
    for tap in range(9):
        out_ref[tap] = jnp.concatenate(
            [held[index, :, tap * slab : (tap + 1) * slab] for index in range(group)], axis=1
        )


def time_end(plan, *refs):
    pieces, out_ref, held = refs[:-2], refs[-2], refs[-1]
    low, high, _ = plan.place()
    group, slab, size = plan.group, plan.slab, plan.thalf
    for d in range(group):
        held[pl.ds(pl.multiple_of(high * size, 16), size), :] = pieces[d][...].astype(F32)
        held[pl.ds(pl.multiple_of((1 - high) * size, 16), size), :] = pieces[d + group][...].astype(F32)
        turned = held[...].T * plan.factor
        for k in range(3):
            here = pl.ds(pl.multiple_of((low ^ d) * slab, 16), slab)
            out_ref[k, here, :] = turned[k * slab : (k + 1) * slab, :]


def per_device(plan, frames, cotangent, w_space, w_time):
    pixels, chans, group, seqs = plan.pixels, plan.chans, plan.group, plan.seqs
    slab, rows, cols = plan.slab, plan.rows, plan.cols
    part = lambda fn: functools.partial(fn, plan)

    def swap(value, distance):
        return lax.ppermute(value, "clip", [(i, i ^ distance) for i in range(plan.clips)])

    def turn(value, k):
        return lax.ppermute(value, "seq", [(i, (i + k) % seqs) for i in range(seqs)])

    clip_f, clip_g = frames.reshape(pixels, chans), cotangent.reshape(pixels, chans)
    own, grad, piece = call(
        part(prepare),
        [((2 * chans, pixels), BF16), ((chans, pixels), BF16), ((rows, cols), BF16)],
        clip_f,
        clip_g,
        jnp.transpose(w_space, (1, 0, 2)),
    )
    before = lax.ppermute(grad, "seq", [(i, i + 1) for i in range(seqs - 1)])
    after = lax.ppermute(grad, "seq", [(i + 1, i) for i in range(seqs - 1)])
    pieces = [piece] + [turn(piece, k) for k in range(1, seqs)]

    def gathered(block):
        pair = swap(block, 2)
        return block, pair, swap(jnp.concatenate([block, pair], axis=0), 1)

    fg = gathered(own)
    halo = gathered(jnp.concatenate([before, after], axis=0))
    lanes = group * pixels
    w_all, f_all, acts, slope = call(
        part(forward),
        [((chans, cols), BF16), ((chans, lanes), BF16), ((slab, lanes), BF16), ((slab, lanes), F32)],
        *pieces,
        *fg,
        scratch=[pltpu.VMEM((cols, lanes), F32)],
    )
    t_send, t_keep = call(
        part(temporal),
        [((plan.thalf, plan.tcols), BF16), ((plan.thalf, plan.tcols), F32)],
        acts,
        *fg,
        *halo,
        scratch=[pltpu.VMEM((chans, plan.tcols), F32)],
    )
    t_got = swap(t_send, group)
    s_send, s_keep, f_send, f_keep = call(
        part(spatial),
        [
            ((chans, plan.half), BF16),
            ((chans, plan.half), F32),
            ((2 * chans, pixels), BF16),
            ((2 * chans, pixels), F32),
        ],
        w_all,
        f_all,
        slope,
        w_time,
        *fg,
        *halo,
        scratch=[pltpu.VMEM((cols, lanes), BF16), pltpu.VMEM((chans, 2 * plan.half), F32)],
    )
    s_got = swap(s_send, group)
    f_got = swap(f_send, 2)

    t_part = (t_keep + t_got.astype(F32)).astype(BF16)
    t_sum = t_keep + t_got.astype(F32)
    for k in range(1, seqs):
        t_sum = t_sum + turn(t_part, k).astype(F32)
    t_sum = t_sum.astype(BF16)

    s_own, *s_parts = call(
        part(space_rows),
        [((rows, plan.half), F32)] + [((rows, plan.half), BF16)] * (seqs - 1),
        s_keep,
        s_got,
        scratch=[pltpu.VMEM((chans, plan.half), F32)],
    )
    s_sum = s_own
    for k in range(1, seqs):
        s_sum = s_sum + turn(s_parts[k - 1], k).astype(F32)
    s_sum = s_sum.astype(BF16)

    f_half, f_own = call(
        part(frame_half), [((chans, pixels), BF16), ((chans, pixels), F32)], f_keep, f_got
    )
    f_other = swap(f_half, 1)
    (f_out,) = call(part(frame_end), [((pixels, chans), BF16)], f_own, f_other, clip_g)

    def everywhere(value):
        held = {0: value}
        for distance in (2, group, group + 2):
            held[distance] = swap(value, distance)
        for distance in (0, 2, group, group + 2):
            held[distance + 1] = swap(held[distance], 1)
        return [held[distance] for distance in range(2 * group)]

    (t_out,) = call(
        part(time_end),
        [((3, chans, chans), F32)],
        *everywhere(t_sum),
        scratch=[pltpu.VMEM((chans, plan.tcols), F32)],
    )
    (s_out,) = call(
        part(space_end),
        [((9, rows, chans), F32)],
        *everywhere(s_sum),
        scratch=[pltpu.VMEM((group, rows, 2 * plan.half), F32)],
    )
    return f_out.reshape(frames.shape), jnp.transpose(s_out, (1, 0, 2)), t_out


def solution(mesh):
    in_specs = (
        P("clip", "seq", None, None, None),
        P("clip", "seq", None, None, None),
        P("seq", None, None),
        P(),
    )
    out_specs = (P("clip", "seq", None, None, None), P("seq", None, None), P())

    def body(frames, cotangent, w_space, w_time):
        one, count, height, width, chans = frames.shape
        plan = Plan(mesh.shape["clip"], mesh.shape["seq"], height, width, chans)
        if one == 1 and count == 1 and plan.fits():
            return per_device(plan, frames, cotangent, w_space, w_time)
        return per_device_general(frames, cotangent, w_space, w_time)

    return jax.shard_map(body, mesh=mesh, in_specs=in_specs, out_specs=out_specs, check_vma=False)
```

```python
import functools
import math

import jax
import jax.numpy as jnp
from jax import lax
from jax.experimental import pallas as pl
from jax.experimental.pallas import tpu as pltpu
from jax.sharding import PartitionSpec as P


def padded_2(cells, sides, width):
    for axis, dim in sides:
        count = lax.axis_size(axis)
        ends = count - 1
        head = lax.slice_in_dim(cells, 0, width, axis=dim)
        tail = lax.slice_in_dim(cells, cells.shape[dim] - width, cells.shape[dim], axis=dim)
        cells = jnp.concatenate(
            [
                lax.ppermute(tail, axis, [(i, (i + 1) % count) for i in range(ends)]),
                cells,
                lax.ppermute(head, axis, [((i + 1) % count, i) for i in range(ends)]),
            ],
            axis=dim,
        )
    return cells


def temporal_grads(acts, g_pad, w_time):
    count = acts.shape[0]
    chans = acts.shape[-1]
    flat_acts = acts.reshape(-1, chans)
    act_grad = jnp.zeros(flat_acts.shape, jnp.float32)
    time_terms = []
    for k in range(3):
        shifted = g_pad[2 - k : 2 - k + count].reshape(-1, chans)
        act_grad = act_grad + lax.dot_general(
            shifted, w_time[k], (((1,), (1,)), ((), ())), preferred_element_type=jnp.float32
        )
        time_terms.append(
            lax.dot_general(
                flat_acts, shifted, (((0,), (0,)), ((), ())), preferred_element_type=jnp.float32
            )
        )
    return (act_grad.astype(jnp.bfloat16).reshape(acts.shape), jnp.stack(time_terms, axis=0))


def per_device_general(frames, cotangent, w_space, w_time):
    weights = lax.all_gather(w_space, "seq", axis=0, tiled=True)
    clip_x = frames[0]
    clip_g = cotangent[0]
    count, height, width, chans = clip_x.shape
    factor = 1.0 / math.sqrt(lax.axis_size("clip") * count * lax.axis_size("seq") * height * width)
    padded = jnp.pad(clip_x, ((0, 0), (1, 1), (1, 1), (0, 0)))
    pieces = [
        padded[:, i : i + height, j : j + width, :].reshape(-1, chans)
        for i in range(3)
        for j in range(3)
    ]
    pre_act = jnp.zeros((count * height * width, chans), jnp.float32)
    for tap in range(9):
        pre_act = pre_act + jnp.dot(
            pieces[tap], weights[:, tap, :], preferred_element_type=jnp.float32
        )
    acts = jax.nn.silu(pre_act).astype(jnp.bfloat16).reshape(1, count, height, width, chans)
    g_rims = padded_2(cotangent, (("seq", 1),), 1)
    g_pad = g_rims[0].reshape(count + 2, height * width, chans)
    act_grad, time_terms = temporal_grads(
        acts[0].reshape(count, height * width, chans), g_pad, w_time
    )
    sigma = jax.nn.sigmoid(pre_act)
    pre_grad = (
        act_grad.reshape(-1, chans).astype(jnp.float32) * sigma * (1.0 + pre_act * (1.0 - sigma))
    ).astype(jnp.bfloat16)
    terms = []
    for tap in range(9):
        part = pieces[tap]
        terms.append(
            lax.dot_general(
                part, pre_grad, (((0,), (0,)), ((), ())), preferred_element_type=jnp.float32
            )
        )
    space_share = lax.psum_scatter(
        jnp.stack(terms, axis=1) * factor, "seq", scatter_dimension=0, tiled=True
    )
    space_grad = lax.psum(space_share, "clip")
    time_grad = lax.psum(time_terms * factor, ("clip", "seq"))
    grad_pad = jnp.pad(
        pre_grad.reshape(count, height, width, chans), ((0, 0), (1, 1), (1, 1), (0, 0))
    )
    input_grad = clip_g.reshape(-1, chans).astype(jnp.float32)
    for i in range(3):
        for j in range(3):
            piece = grad_pad[:, 2 - i : 2 - i + height, 2 - j : 2 - j + width, :].reshape(-1, chans)
            input_grad = input_grad + lax.dot_general(
                piece,
                weights[:, 3 * i + j, :],
                (((1,), (1,)), ((), ())),
                preferred_element_type=jnp.float32,
            )
    frames_grad = input_grad.astype(jnp.bfloat16).reshape(1, count, height, width, chans)
    return (frames_grad, space_grad, time_grad)


BF16 = jnp.bfloat16
F32 = jnp.float32
LANES = 128
VMEM = pl.BlockSpec(memory_space=pltpu.VMEM)
NN = (((1,), (0,)), ((), ()))
NT = (((1,), (1,)), ((), ()))
TN = (((0,), (0,)), ((), ()))


def round_up(value, unit):
    return -(-value // unit) * unit


def mm(lhs, rhs, dims):
    return lax.dot_general(lhs, rhs, dims, preferred_element_type=F32)


def call(kernel, outs, *args, scratch=()):
    return pl.pallas_call(
        kernel,
        out_shape=tuple(jax.ShapeDtypeStruct(shape, dtype) for shape, dtype in outs),
        in_specs=[VMEM] * len(args),
        out_specs=(VMEM,) * len(outs),
        scratch_shapes=list(scratch),
        compiler_params=pltpu.CompilerParams(vmem_limit_bytes=48 * 1024 * 1024),
    )(*args)


class Plan:
    def __init__(self, clips, seqs, height, width, chans):
        self.clips, self.seqs = clips, seqs
        self.height, self.width, self.chans = height, width, chans
        self.group = clips // 2
        self.slab = chans // max(self.group, 1)
        self.rows = chans // seqs
        self.pixels = height * width
        self.cols = 9 * self.slab
        self.half = round_up(round_up(self.cols, 2 * LANES) // 2, LANES)
        self.tcols = round_up(3 * self.slab, LANES)
        self.thalf = chans // 2
        self.factor = 1.0 / math.sqrt(clips * seqs * self.pixels)

    def fits(self):
        return (
            self.group == 4
            and self.slab * self.group == self.chans
            and self.rows * self.seqs == self.chans
            and self.slab % 16 == 0
            and self.rows % 16 == 0
            and self.thalf % 16 == 0
            and self.pixels % LANES == 0
            and self.seqs >= 2
        )

    def place(self):
        clip = lax.axis_index("clip")
        return clip % self.group, clip // self.group, lax.axis_index("seq")


def prepare(plan, f_hbm, g_hbm, w_hbm, fg_ref, gt_ref, wp_ref, wh_ref, f_ref, g_ref, w_ref, sems):
    low, high, _ = plan.place()
    chans, slab, half = plan.chans, plan.slab, plan.half
    copies = [
        pltpu.make_async_copy(src, dst, sems.at[index])
        for index, (src, dst) in enumerate(((g_hbm, g_ref), (w_hbm, w_ref), (f_hbm, f_ref)))
    ]
    for copy in copies:
        copy.start()
    copies[0].wait()
    grad = g_ref[...].T
    gt_ref[...] = grad
    fg_ref[chans:, :] = grad
    copies[1].wait()
    for index in range(plan.group):

        @pl.when(low == index)
        def _():
            taps = [w_ref[tap][:, slab * index : slab * (index + 1)] for tap in range(9)]
            if plan.cols < 2 * half:
                taps.append(jnp.zeros((plan.rows, 2 * half - plan.cols), BF16))
            wp_ref[...] = jnp.concatenate(taps, axis=1)

    wh_ref[...] = wp_ref[:, pl.ds(pl.multiple_of(high * half, LANES), half)]
    copies[2].wait()
    fg_ref[:chans, :] = f_ref[...].T


def shifts(plan, lanes):
    lane = lax.broadcasted_iota(jnp.int32, (1, lanes), 1) % plan.pixels
    row, col = lane // plan.width, lane % plan.width
    found = []
    for i in range(3):
        for j in range(3):
            inside = (
                (row + (i - 1) >= 0)
                & (row + (i - 1) < plan.height)
                & (col + (j - 1) >= 0)
                & (col + (j - 1) < plan.width)
            )
            found.append(((i - 1) * plan.width + (j - 1), inside))
    return found


def rolled(value, distance):
    lanes = value.shape[1]
    return value if distance == 0 else pltpu.roll(value, (-distance) % lanes, 1)


def group_frames(plan, own_ref, pair_ref, core_ref, part):
    chans = plan.chans
    first = slice(part * chans, (part + 1) * chans)
    second = slice((2 + part) * chans, (3 + part) * chans)
    return [own_ref[first, :], core_ref[first, :], pair_ref[first, :], core_ref[second, :]]


def weights(plan, *refs):
    own_ref, got_refs, other_ref = refs[0], refs[1 : plan.seqs], refs[plan.seqs]
    mine_ref, pair_ref, w_all, w_turned, both_ref = refs[plan.seqs + 1 :]
    _, high, z = plan.place()
    rows, half = plan.rows, plan.half
    here = pl.ds(pl.multiple_of(high * half, LANES), half)
    there = pl.ds(pl.multiple_of((1 - high) * half, LANES), half)
    w_all[pl.ds(pl.multiple_of(z * rows, 16), rows), :] = own_ref[...]
    for k, got_ref in enumerate(got_refs, 1):
        place = pl.ds(pl.multiple_of((z - k + plan.seqs) % plan.seqs * rows, 16), rows)
        w_all[place, here] = got_ref[...]
        w_all[place, there] = other_ref[(k - 1) * rows : k * rows, :]
    w_turned[...] = w_all[...].T
    both_ref[: 2 * plan.chans, :] = mine_ref[...]
    both_ref[2 * plan.chans :, :] = pair_ref[...]


def forward(plan, w_turned, own_ref, pair_ref, core_ref, f_all, a_ref, d_ref, taps):
    slab = plan.slab
    for d, frame in enumerate(group_frames(plan, own_ref, pair_ref, core_ref, 0)):
        f_all[:, d * plan.pixels : (d + 1) * plan.pixels] = frame
    taps[...] = mm(w_turned[: plan.cols, :], f_all[...], NN)
    total = None
    for tap, (distance, inside) in enumerate(shifts(plan, f_all.shape[1])):
        term = rolled(taps[tap * slab : (tap + 1) * slab, :], distance)
        term = jnp.where(inside, term, 0.0)
        total = term if total is None else total + term
    sigma = 1.0 / (1.0 + jnp.exp(-total))
    a_ref[...] = (total * sigma).astype(BF16)
    d_ref[...] = sigma * (1.0 + total * (1.0 - sigma))


def cotangents(plan, fg_refs, halo_refs):
    before = group_frames(plan, *halo_refs, 0)
    after = group_frames(plan, *halo_refs, 1)
    here = group_frames(plan, *fg_refs, 1)
    return [after, here, before]


def temporal(plan, a_ref, *refs):
    fg_refs, halo_refs = refs[:3], refs[3:6]
    send_ref, keep_ref, total = refs[6:]
    _, high, _ = plan.place()
    pixels = plan.pixels
    acts = a_ref[...]
    parts = []
    for grads in cotangents(plan, fg_refs, halo_refs):
        term = None
        for d, grad in enumerate(grads):
            here = mm(grad, acts[:, d * pixels : (d + 1) * pixels], NT)
            term = here if term is None else term + here
        parts.append(term)
    pad = plan.tcols - 3 * plan.slab
    if pad:
        parts.append(jnp.zeros((plan.chans, pad), F32))
    total[...] = jnp.concatenate(parts, axis=1)
    size = plan.thalf
    keep_ref[...] = total[pl.ds(pl.multiple_of(high * size, 16), size), :]
    send_ref[...] = total[pl.ds(pl.multiple_of((1 - high) * size, 16), size), :].astype(BF16)


def spatial(plan, *refs):
    w_all, f_all, d_ref, wt_ref = refs[:4]
    fg_refs, halo_refs = refs[4:7], refs[7:10]
    s_send, s_keep, f_send, f_keep, expanded, total = refs[10:]
    low, high, _ = plan.place()
    pixels, slab, chans = plan.pixels, plan.slab, plan.chans
    parts = [None] * plan.group
    for k, grads in enumerate(cotangents(plan, fg_refs, halo_refs)):
        weight = wt_ref[k, pl.ds(pl.multiple_of(low * slab, 16), slab), :]
        for d, grad in enumerate(grads):
            here = mm(weight, grad, NN)
            parts[d] = here if parts[d] is None else parts[d] + here
    act_grad = jnp.concatenate(parts, axis=1).astype(BF16).astype(F32)
    pre_grad = (act_grad * d_ref[...]).astype(BF16).astype(F32)
    for tap, (distance, _) in enumerate(shifts(plan, pre_grad.shape[1])):
        inside = shifts(plan, pre_grad.shape[1])[8 - tap][1]
        term = jnp.where(inside, rolled(pre_grad, -distance), 0.0)
        expanded[tap * slab : (tap + 1) * slab, :] = term.astype(BF16)
    total[:, : plan.cols] = mm(f_all[...], expanded[...], NT)
    if plan.cols < total.shape[1]:
        total[:, plan.cols :] = jnp.zeros((chans, total.shape[1] - plan.cols), F32)
    size = plan.half
    s_keep[...] = total[:, pl.ds(pl.multiple_of(high * size, LANES), size)]
    s_send[...] = total[:, pl.ds(pl.multiple_of((1 - high) * size, LANES), size)].astype(BF16)
    grads = mm(w_all[:, : plan.cols], expanded[...], NN)
    for d in range(2):
        f_keep[d * chans : (d + 1) * chans, :] = grads[:, d * pixels : (d + 1) * pixels]
        there = grads[:, (2 + d) * pixels : (3 + d) * pixels]
        f_send[d * chans : (d + 1) * chans, :] = there.astype(BF16)


def time_rows(plan, keep_ref, got_ref, after_ref, own_ref, send_ref):
    total = keep_ref[...] + got_ref[...].astype(F32)
    own_ref[...] = total
    send_ref[...] = total.astype(BF16)


def frame_half(plan, keep_ref, got_ref, send_ref, own_ref):
    chans = plan.chans
    own_ref[...] = keep_ref[:chans, :] + got_ref[:chans, :].astype(F32)
    send_ref[...] = (keep_ref[chans:, :] + got_ref[chans:, :].astype(F32)).astype(BF16)


def frame_end(plan, own_ref, got_ref, g_ref, out_ref):
    total = own_ref[...] + got_ref[...].astype(F32)
    out_ref[...] = (g_ref[...].astype(F32) + total.T).astype(BF16)


def space_rows(plan, keep_ref, got_ref, *refs):
    own_ref, send_refs, total = refs[0], refs[1:-1], refs[-1]
    _, _, z = plan.place()
    total[...] = keep_ref[...] + got_ref[...].astype(F32)
    rows = plan.rows
    own_ref[...] = total[pl.ds(pl.multiple_of(z * rows, 16), rows), :]
    for k, ref in enumerate(send_refs, 1):
        other = (z + k) % plan.seqs
        ref[...] = total[pl.ds(pl.multiple_of(other * rows, 16), rows), :].astype(BF16)


def space_end(plan, *refs):
    pieces, out_ref, held = refs[:-2], refs[-2], refs[-1]
    low, high, _ = plan.place()
    group, slab = plan.group, plan.slab
    for m, piece in enumerate(pieces):
        other = high if m < group else 1 - high
        lane = pl.multiple_of(other * plan.half, LANES)
        held[low ^ (m % group), :, pl.ds(lane, plan.half)] = piece[...].astype(F32) * plan.factor
    for tap in range(9):
        out_ref[tap] = jnp.concatenate(
            [held[index, :, tap * slab : (tap + 1) * slab] for index in range(group)], axis=1
        )


def time_end(plan, *refs):
    pieces, out_ref, held = refs[:-2], refs[-2], refs[-1]
    low, high, _ = plan.place()
    group, slab, size = plan.group, plan.slab, plan.thalf
    for d in range(group):
        held[pl.ds(pl.multiple_of(high * size, 16), size), :] = pieces[d][...].astype(F32)
        held[pl.ds(pl.multiple_of((1 - high) * size, 16), size), :] = pieces[d + group][...].astype(F32)
        turned = held[...].T * plan.factor
        for k in range(3):
            here = pl.ds(pl.multiple_of((low ^ d) * slab, 16), slab)
            out_ref[k, here, :] = turned[k * slab : (k + 1) * slab, :]


def per_device(plan, frames, cotangent, w_space, w_time):
    pixels, chans, group, seqs = plan.pixels, plan.chans, plan.group, plan.seqs
    slab, rows, cols = plan.slab, plan.rows, plan.cols
    part = lambda fn: functools.partial(fn, plan)

    def swap(value, distance):
        return lax.ppermute(value, "clip", [(i, i ^ distance) for i in range(plan.clips)])

    def neighbours(value):
        z = lax.axis_index("seq")
        found = []
        for first in range(2):
            other = {i: i for i in range(seqs)}
            for i in range(first, seqs - 1, 2):
                other[i], other[i + 1] = i + 1, i
            found.append(lax.ppermute(value, "seq", list(other.items())))
        low, high = jnp.where(z % 2 == 1, *found), jnp.where(z % 2 == 1, *found[::-1])
        zero = jnp.zeros_like(value)
        return jnp.where(z == 0, zero, low), jnp.where(z == seqs - 1, zero, high)

    def turn(value, k):
        return lax.ppermute(value, "seq", [(i, (i + k) % seqs) for i in range(seqs)])

    clip_f, clip_g = frames.reshape(pixels, chans), cotangent.reshape(pixels, chans)
    taps = jnp.transpose(w_space, (1, 0, 2))
    outs = [
        ((2 * chans, pixels), BF16),
        ((chans, pixels), BF16),
        ((rows, 2 * plan.half), BF16),
        ((rows, plan.half), BF16),
    ]
    own, grad, piece, part_piece = pl.pallas_call(
        part(prepare),
        out_shape=tuple(jax.ShapeDtypeStruct(shape, dtype) for shape, dtype in outs),
        in_specs=[pl.BlockSpec(memory_space=pl.ANY)] * 3,
        out_specs=(VMEM,) * len(outs),
        scratch_shapes=[
            pltpu.VMEM(clip_f.shape, BF16),
            pltpu.VMEM(clip_g.shape, BF16),
            pltpu.VMEM(taps.shape, BF16),
            pltpu.SemaphoreType.DMA((3,)),
        ],
    )(clip_f, clip_g, taps)
    before, after = neighbours(grad)
    got = [turn(part_piece, k) for k in range(1, seqs)]
    other = swap(jnp.concatenate(got, axis=0), group)
    pair = swap(own, 2)
    w_all, w_turned, both = call(
        part(weights),
        [((chans, 2 * plan.half), BF16), ((2 * plan.half, chans), BF16), ((4 * chans, pixels), BF16)],
        piece,
        *got,
        other,
        own,
        pair,
    )
    fg = (own, pair, swap(both, 1))
    halo_own = jnp.concatenate([before, after], axis=0)
    halo_pair = swap(halo_own, 2)
    halo = (halo_own, halo_pair, swap(jnp.concatenate([halo_own, halo_pair], axis=0), 1))
    lanes = group * pixels
    f_all, acts, slope = call(
        part(forward),
        [((chans, lanes), BF16), ((slab, lanes), BF16), ((slab, lanes), F32)],
        w_turned,
        *fg,
        scratch=[pltpu.VMEM((cols, lanes), F32)],
    )
    t_send, t_keep = call(
        part(temporal),
        [((plan.thalf, plan.tcols), BF16), ((plan.thalf, plan.tcols), F32)],
        acts,
        *fg,
        *halo,
        scratch=[pltpu.VMEM((chans, plan.tcols), F32)],
    )
    t_got = swap(t_send, group)
    s_send, s_keep, f_send, f_keep = call(
        part(spatial),
        [
            ((chans, plan.half), BF16),
            ((chans, plan.half), F32),
            ((2 * chans, pixels), BF16),
            ((2 * chans, pixels), F32),
        ],
        w_all,
        f_all,
        slope,
        w_time,
        *fg,
        *halo,
        scratch=[pltpu.VMEM((cols, lanes), BF16), pltpu.VMEM((chans, 2 * plan.half), F32)],
    )
    s_got = swap(s_send, group)
    f_got = swap(f_send, 2)

    t_sum, t_part = call(
        part(time_rows), [(t_keep.shape, F32), (t_keep.shape, BF16)], t_keep, t_got, s_send
    )
    for k in range(1, seqs):
        t_sum = t_sum + turn(t_part, k).astype(F32)
    t_sum = t_sum.astype(BF16)

    s_own, *s_parts = call(
        part(space_rows),
        [((rows, plan.half), F32)] + [((rows, plan.half), BF16)] * (seqs - 1),
        s_keep,
        s_got,
        scratch=[pltpu.VMEM((chans, plan.half), F32)],
    )
    s_sum = s_own
    for k in range(1, seqs):
        s_sum = s_sum + turn(s_parts[k - 1], k).astype(F32)
    s_sum = s_sum.astype(BF16)

    f_half, f_own = call(
        part(frame_half), [((chans, pixels), BF16), ((chans, pixels), F32)], f_keep, f_got
    )
    f_other = swap(f_half, 1)
    (f_out,) = call(part(frame_end), [((pixels, chans), BF16)], f_own, f_other, clip_g)

    def everywhere(value):
        held = {0: value}
        for distance in (2, group, group + 2):
            held[distance] = swap(value, distance)
        for distance in (0, 2, group, group + 2):
            held[distance + 1] = swap(held[distance], 1)
        return [held[distance] for distance in range(2 * group)]

    (t_out,) = call(
        part(time_end),
        [((3, chans, chans), F32)],
        *everywhere(t_sum),
        scratch=[pltpu.VMEM((chans, plan.tcols), F32)],
    )
    (s_out,) = call(
        part(space_end),
        [((9, rows, chans), F32)],
        *everywhere(s_sum),
        scratch=[pltpu.VMEM((group, rows, 2 * plan.half), F32)],
    )
    return f_out.reshape(frames.shape), jnp.transpose(s_out, (1, 0, 2)), t_out


def solution(mesh):
    in_specs = (
        P("clip", "seq", None, None, None),
        P("clip", "seq", None, None, None),
        P("seq", None, None),
        P(),
    )
    out_specs = (P("clip", "seq", None, None, None), P("seq", None, None), P())

    def body(frames, cotangent, w_space, w_time):
        one, count, height, width, chans = frames.shape
        plan = Plan(mesh.shape["clip"], mesh.shape["seq"], height, width, chans)
        if one == 1 and count == 1 and plan.fits():
            return per_device(plan, frames, cotangent, w_space, w_time)
        return per_device_general(frames, cotangent, w_space, w_time)

    return jax.shard_map(body, mesh=mesh, in_specs=in_specs, out_specs=out_specs, check_vma=False)
```

```python
import functools
import math

import jax
import jax.numpy as jnp
from jax import lax
from jax.experimental import pallas as pl
from jax.experimental.pallas import tpu as pltpu
from jax.sharding import PartitionSpec as P


def padded_2(cells, sides, width):
    for axis, dim in sides:
        count = lax.axis_size(axis)
        ends = count - 1
        head = lax.slice_in_dim(cells, 0, width, axis=dim)
        tail = lax.slice_in_dim(cells, cells.shape[dim] - width, cells.shape[dim], axis=dim)
        cells = jnp.concatenate(
            [
                lax.ppermute(tail, axis, [(i, (i + 1) % count) for i in range(ends)]),
                cells,
                lax.ppermute(head, axis, [((i + 1) % count, i) for i in range(ends)]),
            ],
            axis=dim,
        )
    return cells


def temporal_grads(acts, g_pad, w_time):
    count = acts.shape[0]
    chans = acts.shape[-1]
    flat_acts = acts.reshape(-1, chans)
    act_grad = jnp.zeros(flat_acts.shape, jnp.float32)
    time_terms = []
    for k in range(3):
        shifted = g_pad[2 - k : 2 - k + count].reshape(-1, chans)
        act_grad = act_grad + lax.dot_general(
            shifted, w_time[k], (((1,), (1,)), ((), ())), preferred_element_type=jnp.float32
        )
        time_terms.append(
            lax.dot_general(
                flat_acts, shifted, (((0,), (0,)), ((), ())), preferred_element_type=jnp.float32
            )
        )
    return (act_grad.astype(jnp.bfloat16).reshape(acts.shape), jnp.stack(time_terms, axis=0))


def per_device_general(frames, cotangent, w_space, w_time):
    weights = lax.all_gather(w_space, "seq", axis=0, tiled=True)
    clip_x = frames[0]
    clip_g = cotangent[0]
    count, height, width, chans = clip_x.shape
    factor = 1.0 / math.sqrt(lax.axis_size("clip") * count * lax.axis_size("seq") * height * width)
    padded = jnp.pad(clip_x, ((0, 0), (1, 1), (1, 1), (0, 0)))
    pieces = [
        padded[:, i : i + height, j : j + width, :].reshape(-1, chans)
        for i in range(3)
        for j in range(3)
    ]
    pre_act = jnp.zeros((count * height * width, chans), jnp.float32)
    for tap in range(9):
        pre_act = pre_act + jnp.dot(
            pieces[tap], weights[:, tap, :], preferred_element_type=jnp.float32
        )
    acts = jax.nn.silu(pre_act).astype(jnp.bfloat16).reshape(1, count, height, width, chans)
    g_rims = padded_2(cotangent, (("seq", 1),), 1)
    g_pad = g_rims[0].reshape(count + 2, height * width, chans)
    act_grad, time_terms = temporal_grads(
        acts[0].reshape(count, height * width, chans), g_pad, w_time
    )
    sigma = jax.nn.sigmoid(pre_act)
    pre_grad = (
        act_grad.reshape(-1, chans).astype(jnp.float32) * sigma * (1.0 + pre_act * (1.0 - sigma))
    ).astype(jnp.bfloat16)
    terms = []
    for tap in range(9):
        part = pieces[tap]
        terms.append(
            lax.dot_general(
                part, pre_grad, (((0,), (0,)), ((), ())), preferred_element_type=jnp.float32
            )
        )
    space_share = lax.psum_scatter(
        jnp.stack(terms, axis=1) * factor, "seq", scatter_dimension=0, tiled=True
    )
    space_grad = lax.psum(space_share, "clip")
    time_grad = lax.psum(time_terms * factor, ("clip", "seq"))
    grad_pad = jnp.pad(
        pre_grad.reshape(count, height, width, chans), ((0, 0), (1, 1), (1, 1), (0, 0))
    )
    input_grad = clip_g.reshape(-1, chans).astype(jnp.float32)
    for i in range(3):
        for j in range(3):
            piece = grad_pad[:, 2 - i : 2 - i + height, 2 - j : 2 - j + width, :].reshape(-1, chans)
            input_grad = input_grad + lax.dot_general(
                piece,
                weights[:, 3 * i + j, :],
                (((1,), (1,)), ((), ())),
                preferred_element_type=jnp.float32,
            )
    frames_grad = input_grad.astype(jnp.bfloat16).reshape(1, count, height, width, chans)
    return (frames_grad, space_grad, time_grad)


BF16 = jnp.bfloat16
F32 = jnp.float32
LANES = 128
VMEM = pl.BlockSpec(memory_space=pltpu.VMEM)
NN = (((1,), (0,)), ((), ()))
NT = (((1,), (1,)), ((), ()))
TN = (((0,), (0,)), ((), ()))


def round_up(value, unit):
    return -(-value // unit) * unit


def mm(lhs, rhs, dims):
    return lax.dot_general(lhs, rhs, dims, preferred_element_type=F32)


def call(kernel, outs, *args, after=(), scratch=()):
    def body(*refs):
        kernel(*refs[: len(args)], *refs[len(args) + len(after) :])

    return pl.pallas_call(
        body,
        out_shape=tuple(jax.ShapeDtypeStruct(shape, dtype) for shape, dtype in outs),
        in_specs=[VMEM] * len(args) + [pl.BlockSpec(memory_space=pl.ANY)] * len(after),
        out_specs=(VMEM,) * len(outs),
        scratch_shapes=list(scratch),
        compiler_params=pltpu.CompilerParams(vmem_limit_bytes=48 * 1024 * 1024),
    )(*args, *after)


class Plan:
    def __init__(self, clips, seqs, height, width, chans):
        self.clips, self.seqs = clips, seqs
        self.height, self.width, self.chans = height, width, chans
        self.group = clips // 2
        self.slab = chans // max(self.group, 1)
        self.rows = chans // seqs
        self.pixels = height * width
        self.cols = 9 * self.slab
        self.half = round_up(round_up(self.cols, 2 * LANES) // 2, LANES)
        self.tcols = round_up(3 * self.slab, LANES)
        self.thalf = chans // 2
        self.factor = 1.0 / math.sqrt(clips * seqs * self.pixels)

    def fits(self):
        return (
            self.group == 4
            and self.slab * self.group == self.chans
            and self.rows * self.seqs == self.chans
            and self.slab % 16 == 0
            and self.rows % 16 == 0
            and self.thalf % 16 == 0
            and self.pixels % LANES == 0
            and self.seqs == 4
        )

    def place(self):
        clip = lax.axis_index("clip")
        return clip % self.group, clip // self.group, lax.axis_index("seq")


def prepare(plan, f_hbm, g_hbm, w_hbm, ft_ref, gt_ref, wp_ref, wh_ref, f_ref, g_ref, w_ref, sems):
    low, high, _ = plan.place()
    slab, half = plan.slab, plan.half
    copies = [
        pltpu.make_async_copy(src, dst, sems.at[index])
        for index, (src, dst) in enumerate(((g_hbm, g_ref), (w_hbm, w_ref), (f_hbm, f_ref)))
    ]
    for copy in copies:
        copy.start()
    copies[0].wait()
    gt_ref[...] = g_ref[...].T
    copies[1].wait()
    for index in range(plan.group):

        @pl.when(low == index)
        def _():
            taps = [w_ref[tap][:, slab * index : slab * (index + 1)] for tap in range(9)]
            if plan.cols < 2 * half:
                taps.append(jnp.zeros((plan.rows, 2 * half - plan.cols), BF16))
            wp_ref[...] = jnp.concatenate(taps, axis=1)

    wh_ref[...] = wp_ref[:, pl.ds(pl.multiple_of(high * half, LANES), half)]
    copies[2].wait()
    ft_ref[...] = f_ref[...].T


def shifts(plan, lanes):
    lane = lax.broadcasted_iota(jnp.int32, (1, lanes), 1) % plan.pixels
    row, col = lane // plan.width, lane % plan.width
    found = []
    for i in range(3):
        for j in range(3):
            inside = (
                (row + (i - 1) >= 0)
                & (row + (i - 1) < plan.height)
                & (col + (j - 1) >= 0)
                & (col + (j - 1) < plan.width)
            )
            found.append(((i - 1) * plan.width + (j - 1), inside))
    return found


def rolled(value, distance):
    lanes = value.shape[1]
    return value if distance == 0 else pltpu.roll(value, (-distance) % lanes, 1)


def weights(plan, *refs):
    own_ref, got_refs, other_ref = refs[0], refs[1 : plan.seqs], refs[plan.seqs]
    w_all, w_turned = refs[plan.seqs + 1 :]
    _, high, z = plan.place()
    rows, half = plan.rows, plan.half
    here = pl.ds(pl.multiple_of(high * half, LANES), half)
    there = pl.ds(pl.multiple_of((1 - high) * half, LANES), half)
    w_all[pl.ds(pl.multiple_of(z * rows, 16), rows), :] = own_ref[...]
    for k, got_ref in enumerate(got_refs, 1):
        place = pl.ds(pl.multiple_of((z - k + plan.seqs) % plan.seqs * rows, 16), rows)
        w_all[place, here] = got_ref[...]
        w_all[place, there] = other_ref[(k - 1) * rows : k * rows, :]
    w_turned[...] = w_all[...].T


def forward(plan, w_turned, *refs):
    slab = plan.slab
    frames, (f_all, a_ref, d_ref, taps) = refs[: plan.group], refs[plan.group :]
    for d, frame in enumerate(frames):
        f_all[:, d * plan.pixels : (d + 1) * plan.pixels] = frame[...]
    taps[...] = mm(w_turned[: plan.cols, :], f_all[...], NN)
    total = None
    for tap, (distance, inside) in enumerate(shifts(plan, f_all.shape[1])):
        term = rolled(taps[tap * slab : (tap + 1) * slab, :], distance)
        term = jnp.where(inside, term, 0.0)
        total = term if total is None else total + term
    sigma = 1.0 / (1.0 + jnp.exp(-total))
    a_ref[...] = (total * sigma).astype(BF16)
    d_ref[...] = sigma * (1.0 + total * (1.0 - sigma))


def act_grads(plan, before_ref, own_ref, after_ref, wt_ref, send_ref, mine_ref, core_ref, total):
    low, _, _ = plan.place()
    slab = plan.slab
    here = mm(wt_ref[0], after_ref[...], NN)
    here = here + mm(wt_ref[1], own_ref[...], NN)
    here = here + mm(wt_ref[2], before_ref[...], NN)
    total[...] = here.astype(BF16)
    for d, ref in enumerate((mine_ref, core_ref)):
        place = slice(d * slab, (d + 1) * slab)
        ref[...] = total[pl.ds(pl.multiple_of((low ^ d) * slab, 16), slab), :]
        send_ref[place, :] = total[pl.ds(pl.multiple_of((low ^ (d + 2)) * slab, 16), slab), :]


def temporal(plan, a_ref, *refs):
    group, pixels, chans = plan.group, plan.pixels, plan.chans
    here_refs, halo_refs = refs[:group], refs[group : 2 * group]
    send_ref, keep_ref, total = refs[2 * group :]
    _, high, _ = plan.place()
    acts = a_ref[...]
    after = [ref[chans:, :] for ref in halo_refs]
    before = [ref[:chans, :] for ref in halo_refs]
    parts = []
    for grads in (after, [ref[...] for ref in here_refs], before):
        term = None
        for d in range(group):
            here = mm(grads[d], acts[:, d * pixels : (d + 1) * pixels], NT)
            term = here if term is None else term + here
        parts.append(term)
    if plan.tcols > 3 * plan.slab:
        parts.append(jnp.zeros((chans, plan.tcols - 3 * plan.slab), F32))
    total[...] = jnp.concatenate(parts, axis=1)
    size = plan.thalf
    keep_ref[...] = total[pl.ds(pl.multiple_of(high * size, 16), size), :]
    send_ref[...] = total[pl.ds(pl.multiple_of((1 - high) * size, 16), size), :].astype(BF16)


def spatial(plan, w_all, f_all, d_ref, mine_ref, core_ref, pair_ref, last_ref, *refs):
    s_send, s_keep, f_send, f_keep, expanded, total = refs
    _, high, _ = plan.place()
    pixels, slab, chans = plan.pixels, plan.slab, plan.chans
    parts = [mine_ref[...], core_ref[...], pair_ref[:slab, :], last_ref[...]]
    parts = [part.astype(F32) for part in parts]
    act_grad = jnp.concatenate(parts, axis=1)
    pre_grad = (act_grad * d_ref[...]).astype(BF16).astype(F32)
    moves = shifts(plan, pre_grad.shape[1])
    for tap, (distance, _) in enumerate(moves):
        inside = moves[8 - tap][1]
        term = jnp.where(inside, rolled(pre_grad, -distance), 0.0)
        expanded[tap * slab : (tap + 1) * slab, :] = term.astype(BF16)
    total[:, : plan.cols] = mm(f_all[...], expanded[...], NT)
    if plan.cols < total.shape[1]:
        total[:, plan.cols :] = jnp.zeros((chans, total.shape[1] - plan.cols), F32)
    size = plan.half
    s_keep[...] = total[:, pl.ds(pl.multiple_of(high * size, LANES), size)]
    s_send[...] = total[:, pl.ds(pl.multiple_of((1 - high) * size, LANES), size)].astype(BF16)
    grads = mm(w_all[:, : plan.cols], expanded[...], NN)
    for index in range(2):
        d = 2 * index
        here = slice(index * chans, (index + 1) * chans)
        f_keep[here, :] = grads[:, d * pixels : (d + 1) * pixels]
        f_send[here, :] = grads[:, (d + 1) * pixels : (d + 2) * pixels].astype(BF16)


def added(keep_ref, got_ref, own_ref, send_ref):
    total = keep_ref[...] + got_ref[...].astype(F32)
    own_ref[...] = total
    send_ref[...] = total.astype(BF16)


def space_halves(plan, keep_ref, got_ref, own_ref, send_ref, total):
    _, _, z = plan.place()
    rows = plan.rows
    total[...] = keep_ref[...] + got_ref[...].astype(F32)
    for n in range(2):
        place = slice(n * rows, (n + 1) * rows)
        own_ref[place, :] = total[pl.ds(pl.multiple_of((z ^ (2 * n)) * rows, 16), rows), :]
        send_ref[place, :] = total[pl.ds(pl.multiple_of((z ^ (2 * n + 1)) * rows, 16), rows), :].astype(BF16)


def space_quarter(plan, keep_ref, got_ref, own_ref, send_ref):
    rows = plan.rows
    own_ref[...] = keep_ref[:rows, :] + got_ref[:rows, :].astype(F32)
    send_ref[...] = (keep_ref[rows:, :] + got_ref[rows:, :].astype(F32)).astype(BF16)


def summed(own_ref, *refs):
    total = own_ref[...]
    for ref in refs[:-1]:
        total = total + ref[...].astype(F32)
    refs[-1][...] = total.astype(BF16)


def stacked(*refs):
    out_ref, first = refs[-1], 0
    for ref in refs[:-1]:
        out_ref[first : first + ref.shape[0], :] = ref[...]
        first += ref.shape[0]


def frame_half(plan, keep_ref, got_ref, send_ref, own_ref):
    chans = plan.chans
    own_ref[...] = keep_ref[:chans, :] + got_ref[:chans, :].astype(F32)
    send_ref[...] = (keep_ref[chans:, :] + got_ref[chans:, :].astype(F32)).astype(BF16)


def ends(plan, t_own, t_got, *refs):
    chips, (f_own, f_got, g_ref, t_sum, s_all, f_out) = refs[:4], refs[4:]
    summed(t_own, t_got, t_sum)
    stacked(*chips, s_all)
    total = f_own[...] + f_got[...].astype(F32)
    f_out[...] = (g_ref[...].astype(F32) + total.T).astype(BF16)


def space_end(plan, here_ref, core_ref, out_ref, token_ref, held):
    low, high, _ = plan.place()
    group, slab, rows = plan.group, plan.slab, plan.rows
    for core, ref in enumerate((here_ref, core_ref)):
        for chip in range(4):
            other = high if chip < 2 else 1 - high
            lane = pl.multiple_of(other * plan.half, LANES)
            piece = ref[chip * rows : (chip + 1) * rows, :].astype(F32) * plan.factor
            held[low ^ (2 * (chip % 2) + core), :, pl.ds(lane, plan.half)] = piece
    for tap in range(9):
        out_ref[tap] = jnp.concatenate(
            [held[index, :, tap * slab : (tap + 1) * slab] for index in range(group)], axis=1
        )
    token_ref[...] = jnp.zeros_like(token_ref)


def time_end(plan, here_ref, core_ref, out_ref, held):
    low, high, _ = plan.place()
    slab, size = plan.slab, plan.thalf
    near = pl.ds(pl.multiple_of(high * size, 16), size)
    far = pl.ds(pl.multiple_of((1 - high) * size, 16), size)
    for core, ref in enumerate((here_ref, core_ref)):
        for pair in range(2):
            held[near, :] = ref[pair * size : (pair + 1) * size, :].astype(F32)
            held[far, :] = ref[(2 + pair) * size : (3 + pair) * size, :].astype(F32)
            turned = held[...].T * plan.factor
            for k in range(3):
                here = pl.ds(pl.multiple_of((low ^ (2 * pair + core)) * slab, 16), slab)
                out_ref[k, here, :] = turned[k * slab : (k + 1) * slab, :]


def per_device(plan, frames, cotangent, w_space, w_time):
    pixels, chans, group, seqs = plan.pixels, plan.chans, plan.group, plan.seqs
    slab, rows, half = plan.slab, plan.rows, plan.half
    lanes = group * pixels
    part = lambda fn: functools.partial(fn, plan)

    def swap(value, distance):
        return lax.ppermute(value, "clip", [(i, i ^ distance) for i in range(plan.clips)])

    def trade(value, distance):
        return lax.ppermute(value, "seq", [(i, i ^ distance) for i in range(seqs)])

    def turn(value, k):
        return lax.ppermute(value, "seq", [(i, (i + k) % seqs) for i in range(seqs)])

    def neighbours(value):
        z = lax.axis_index("seq")
        found = []
        for first in range(2):
            other = {i: i for i in range(seqs)}
            for i in range(first, seqs - 1, 2):
                other[i], other[i + 1] = i + 1, i
            found.append(lax.ppermute(value, "seq", list(other.items())))
        low, high = jnp.where(z % 2 == 1, *found), jnp.where(z % 2 == 1, *found[::-1])
        zero = jnp.zeros_like(value)
        return jnp.where(z == 0, zero, low), jnp.where(z == seqs - 1, zero, high)

    def gathered(own, pair):
        return own, swap(own, 1), pair, swap(pair, 1)

    def chips(value):
        return value, swap(value, 2), swap(value, group), swap(value, group + 2)

    clip_f, clip_g = frames.reshape(pixels, chans), cotangent.reshape(pixels, chans)
    taps = jnp.transpose(w_space, (1, 0, 2))
    frame = (chans, pixels)
    outs = [(frame, BF16), (frame, BF16), ((rows, 2 * half), BF16), ((rows, half), BF16)]
    frame_f, frame_g, piece, half_piece = pl.pallas_call(
        part(prepare),
        out_shape=tuple(jax.ShapeDtypeStruct(shape, dtype) for shape, dtype in outs),
        in_specs=[pl.BlockSpec(memory_space=pl.ANY)] * 3,
        out_specs=(VMEM,) * len(outs),
        scratch_shapes=[
            pltpu.VMEM(clip_f.shape, BF16),
            pltpu.VMEM(clip_g.shape, BF16),
            pltpu.VMEM(taps.shape, BF16),
            pltpu.SemaphoreType.DMA((3,)),
        ],
        compiler_params=pltpu.CompilerParams(vmem_limit_bytes=55_900_000),
    )(clip_f, clip_g, taps)

    w_got = [turn(half_piece, k) for k in range(1, seqs)]
    w_other = swap(jnp.concatenate(w_got, axis=0), group)
    pair_f, pair_g = swap(frame_f, 2), swap(frame_g, 2)
    before, after = neighbours(frame_g)
    d_send, d_mine, d_core = call(
        part(act_grads),
        [((2 * slab, pixels), BF16), ((slab, pixels), BF16), ((slab, pixels), BF16)],
        before,
        frame_g,
        after,
        w_time,
        scratch=[pltpu.VMEM(frame, BF16)],
    )
    d_pair = swap(d_send, 2)
    w_all, w_turned = call(
        part(weights),
        [((chans, 2 * half), BF16), ((2 * half, chans), BF16)],
        piece,
        *w_got,
        w_other,
        after=[pair_g],
    )
    (halo,) = call(
        stacked, [((2 * chans, pixels), BF16)], before, after, after=[w_all, d_pair]
    )
    f_all, acts, slope = call(
        part(forward),
        [((chans, lanes), BF16), ((slab, lanes), BF16), ((slab, lanes), F32)],
        w_turned,
        *gathered(frame_f, pair_f),
        after=[d_pair],
        scratch=[pltpu.VMEM((plan.cols, lanes), F32)],
    )
    s_send, s_keep, f_send, f_keep = call(
        part(spatial),
        [
            ((chans, half), BF16),
            ((chans, half), F32),
            ((2 * chans, pixels), BF16),
            ((2 * chans, pixels), F32),
        ],
        w_all,
        f_all,
        slope,
        d_mine,
        swap(d_core, 1),
        d_pair,
        swap(d_pair[slab:], 1),
        scratch=[pltpu.VMEM((plan.cols, lanes), BF16), pltpu.VMEM((chans, 2 * half), F32)],
    )
    time = (plan.thalf, plan.tcols)
    t_send, t_keep = call(
        part(temporal),
        [(time, BF16), (time, F32)],
        acts,
        *gathered(frame_g, pair_g),
        *gathered(halo, swap(halo, 2)),
        scratch=[pltpu.VMEM((chans, plan.tcols), F32)],
    )

    f_half, f_own = call(
        part(frame_half), [(frame, BF16), (frame, F32)], f_keep, swap(f_send, 1)
    )
    f_other = swap(f_half, 2)
    t_own, t_part = call(added, [(time, F32), (time, BF16)], t_keep, swap(t_send, group))
    t_own, t_part2 = call(added, [(time, F32), (time, BF16)], t_own, trade(t_part, 1))
    t_got = trade(t_part2, 2)
    s_own, s_part = call(
        part(space_halves),
        [((2 * rows, half), F32), ((2 * rows, half), BF16)],
        s_keep,
        swap(s_send, group),
        scratch=[pltpu.VMEM((chans, half), F32)],
    )
    s_own, s_part = call(
        part(space_quarter),
        [((rows, half), F32), ((rows, half), BF16)],
        s_own,
        trade(s_part, 1),
        after=[t_part],
    )
    (s_sum,) = call(
        summed, [((rows, half), BF16)], s_own, trade(s_part, 2), after=[f_other]
    )
    t_sum, s_all, f_out = call(
        part(ends),
        [(time, BF16), ((4 * rows, half), BF16), ((pixels, chans), BF16)],
        t_own,
        t_got,
        *chips(s_sum),
        f_own,
        f_other,
        clip_g,
    )
    s_out, token = call(
        part(space_end),
        [((9, rows, chans), F32), ((8, LANES), F32)],
        s_all,
        swap(s_all, 1),
        scratch=[pltpu.VMEM((group, rows, 2 * half), F32)],
    )
    (t_all,) = call(
        stacked, [((4 * plan.thalf, plan.tcols), BF16)], *chips(t_sum), after=[token]
    )
    (t_out,) = call(
        part(time_end),
        [((3, chans, chans), F32)],
        t_all,
        swap(t_all, 1),
        scratch=[pltpu.VMEM((chans, plan.tcols), F32)],
    )
    return f_out.reshape(frames.shape), jnp.transpose(s_out, (1, 0, 2)), t_out


def solution(mesh):
    in_specs = (
        P("clip", "seq", None, None, None),
        P("clip", "seq", None, None, None),
        P("seq", None, None),
        P(),
    )
    out_specs = (P("clip", "seq", None, None, None), P("seq", None, None), P())

    def body(frames, cotangent, w_space, w_time):
        one, count, height, width, chans = frames.shape
        plan = Plan(mesh.shape["clip"], mesh.shape["seq"], height, width, chans)
        if one == 1 and count == 1 and plan.fits():
            return per_device(plan, frames, cotangent, w_space, w_time)
        return per_device_general(frames, cotangent, w_space, w_time)

    return jax.shard_map(body, mesh=mesh, in_specs=in_specs, out_specs=out_specs, check_vma=False)
```

```python
import functools
import math

import jax
import jax.numpy as jnp
from jax import lax
from jax.experimental import pallas as pl
from jax.experimental.pallas import tpu as pltpu
from jax.sharding import PartitionSpec as P


def padded_2(cells, sides, width):
    for axis, dim in sides:
        count = lax.axis_size(axis)
        ends = count - 1
        head = lax.slice_in_dim(cells, 0, width, axis=dim)
        tail = lax.slice_in_dim(cells, cells.shape[dim] - width, cells.shape[dim], axis=dim)
        cells = jnp.concatenate(
            [
                lax.ppermute(tail, axis, [(i, (i + 1) % count) for i in range(ends)]),
                cells,
                lax.ppermute(head, axis, [((i + 1) % count, i) for i in range(ends)]),
            ],
            axis=dim,
        )
    return cells


def temporal_grads(acts, g_pad, w_time):
    count = acts.shape[0]
    chans = acts.shape[-1]
    flat_acts = acts.reshape(-1, chans)
    act_grad = jnp.zeros(flat_acts.shape, jnp.float32)
    time_terms = []
    for k in range(3):
        shifted = g_pad[2 - k : 2 - k + count].reshape(-1, chans)
        act_grad = act_grad + lax.dot_general(
            shifted, w_time[k], (((1,), (1,)), ((), ())), preferred_element_type=jnp.float32
        )
        time_terms.append(
            lax.dot_general(
                flat_acts, shifted, (((0,), (0,)), ((), ())), preferred_element_type=jnp.float32
            )
        )
    return (act_grad.astype(jnp.bfloat16).reshape(acts.shape), jnp.stack(time_terms, axis=0))


def per_device_general(frames, cotangent, w_space, w_time):
    weights = lax.all_gather(w_space, "seq", axis=0, tiled=True)
    clip_x = frames[0]
    clip_g = cotangent[0]
    count, height, width, chans = clip_x.shape
    factor = 1.0 / math.sqrt(lax.axis_size("clip") * count * lax.axis_size("seq") * height * width)
    padded = jnp.pad(clip_x, ((0, 0), (1, 1), (1, 1), (0, 0)))
    pieces = [
        padded[:, i : i + height, j : j + width, :].reshape(-1, chans)
        for i in range(3)
        for j in range(3)
    ]
    pre_act = jnp.zeros((count * height * width, chans), jnp.float32)
    for tap in range(9):
        pre_act = pre_act + jnp.dot(
            pieces[tap], weights[:, tap, :], preferred_element_type=jnp.float32
        )
    acts = jax.nn.silu(pre_act).astype(jnp.bfloat16).reshape(1, count, height, width, chans)
    g_rims = padded_2(cotangent, (("seq", 1),), 1)
    g_pad = g_rims[0].reshape(count + 2, height * width, chans)
    act_grad, time_terms = temporal_grads(
        acts[0].reshape(count, height * width, chans), g_pad, w_time
    )
    sigma = jax.nn.sigmoid(pre_act)
    pre_grad = (
        act_grad.reshape(-1, chans).astype(jnp.float32) * sigma * (1.0 + pre_act * (1.0 - sigma))
    ).astype(jnp.bfloat16)
    terms = []
    for tap in range(9):
        part = pieces[tap]
        terms.append(
            lax.dot_general(
                part, pre_grad, (((0,), (0,)), ((), ())), preferred_element_type=jnp.float32
            )
        )
    space_share = lax.psum_scatter(
        jnp.stack(terms, axis=1) * factor, "seq", scatter_dimension=0, tiled=True
    )
    space_grad = lax.psum(space_share, "clip")
    time_grad = lax.psum(time_terms * factor, ("clip", "seq"))
    grad_pad = jnp.pad(
        pre_grad.reshape(count, height, width, chans), ((0, 0), (1, 1), (1, 1), (0, 0))
    )
    input_grad = clip_g.reshape(-1, chans).astype(jnp.float32)
    for i in range(3):
        for j in range(3):
            piece = grad_pad[:, 2 - i : 2 - i + height, 2 - j : 2 - j + width, :].reshape(-1, chans)
            input_grad = input_grad + lax.dot_general(
                piece,
                weights[:, 3 * i + j, :],
                (((1,), (1,)), ((), ())),
                preferred_element_type=jnp.float32,
            )
    frames_grad = input_grad.astype(jnp.bfloat16).reshape(1, count, height, width, chans)
    return (frames_grad, space_grad, time_grad)


BF16 = jnp.bfloat16
F32 = jnp.float32
LANES = 128
VMEM = pl.BlockSpec(memory_space=pltpu.VMEM)
NN = (((1,), (0,)), ((), ()))
NT = (((1,), (1,)), ((), ()))
TN = (((0,), (0,)), ((), ()))


def round_up(value, unit):
    return -(-value // unit) * unit


def mm(lhs, rhs, dims):
    return lax.dot_general(lhs, rhs, dims, preferred_element_type=F32)


def call(kernel, outs, *args, after=(), scratch=()):
    def body(*refs):
        kernel(*refs[: len(args)], *refs[len(args) + len(after) :])

    return pl.pallas_call(
        body,
        out_shape=tuple(jax.ShapeDtypeStruct(shape, dtype) for shape, dtype in outs),
        in_specs=[VMEM] * len(args) + [pl.BlockSpec(memory_space=pl.ANY)] * len(after),
        out_specs=(VMEM,) * len(outs),
        scratch_shapes=list(scratch),
        compiler_params=pltpu.CompilerParams(vmem_limit_bytes=48 * 1024 * 1024),
    )(*args, *after)


class Plan:
    def __init__(self, clips, seqs, height, width, chans):
        self.clips, self.seqs = clips, seqs
        self.height, self.width, self.chans = height, width, chans
        self.group = clips // 2
        self.slab = chans // max(self.group, 1)
        self.rows = chans // seqs
        self.pixels = height * width
        self.cols = 9 * self.slab
        self.half = round_up(round_up(self.cols, 2 * LANES) // 2, LANES)
        self.tcols = round_up(3 * self.slab, LANES)
        self.thalf = chans // 2
        self.factor = 1.0 / math.sqrt(clips * seqs * self.pixels)

    def fits(self):
        return (
            self.group == 4
            and self.slab * self.group == self.chans
            and self.rows * self.seqs == self.chans
            and self.slab % 16 == 0
            and self.rows % 16 == 0
            and self.thalf % 16 == 0
            and self.pixels % LANES == 0
            and self.seqs == 4
        )

    def place(self):
        clip = lax.axis_index("clip")
        return clip % self.group, clip // self.group, lax.axis_index("seq")


def prepare(plan, f_hbm, g_hbm, w_hbm, ft_ref, gt_ref, wp_ref, wh_ref, f_ref, g_ref, w_ref, sems):
    low, high, _ = plan.place()
    slab, half = plan.slab, plan.half
    copies = [
        pltpu.make_async_copy(src, dst, sems.at[index])
        for index, (src, dst) in enumerate(((g_hbm, g_ref), (w_hbm, w_ref), (f_hbm, f_ref)))
    ]
    for copy in copies:
        copy.start()
    copies[0].wait()
    gt_ref[...] = g_ref[...].T
    copies[1].wait()
    for index in range(plan.group):

        @pl.when(low == index)
        def _():
            taps = [w_ref[tap][:, slab * index : slab * (index + 1)] for tap in range(9)]
            if plan.cols < 2 * half:
                taps.append(jnp.zeros((plan.rows, 2 * half - plan.cols), BF16))
            wp_ref[...] = jnp.concatenate(taps, axis=1)

    wh_ref[...] = wp_ref[:, pl.ds(pl.multiple_of(high * half, LANES), half)]
    copies[2].wait()
    ft_ref[...] = f_ref[...].T


def shifts(plan, lanes):
    lane = lax.broadcasted_iota(jnp.int32, (1, lanes), 1) % plan.pixels
    row, col = lane // plan.width, lane % plan.width
    found = []
    for i in range(3):
        for j in range(3):
            inside = (
                (row + (i - 1) >= 0)
                & (row + (i - 1) < plan.height)
                & (col + (j - 1) >= 0)
                & (col + (j - 1) < plan.width)
            )
            found.append(((i - 1) * plan.width + (j - 1), inside))
    return found


def rolled(value, distance):
    lanes = value.shape[1]
    return value if distance == 0 else pltpu.roll(value, (-distance) % lanes, 1)


def weights(plan, *refs):
    own_ref, got_refs, other_ref = refs[0], refs[1 : plan.seqs], refs[plan.seqs]
    w_all, w_turned = refs[plan.seqs + 1 :]
    _, high, z = plan.place()
    rows, half = plan.rows, plan.half
    here = pl.ds(pl.multiple_of(high * half, LANES), half)
    there = pl.ds(pl.multiple_of((1 - high) * half, LANES), half)
    w_all[pl.ds(pl.multiple_of(z * rows, 16), rows), :] = own_ref[...]
    for k, got_ref in enumerate(got_refs, 1):
        place = pl.ds(pl.multiple_of((z - k + plan.seqs) % plan.seqs * rows, 16), rows)
        w_all[place, here] = got_ref[...]
        w_all[place, there] = other_ref[(k - 1) * rows : k * rows, :]
    w_turned[...] = w_all[...].T


def forward(plan, w_turned, *refs):
    slab = plan.slab
    frames, (f_all, a_ref, d_ref, taps) = refs[: plan.group], refs[plan.group :]
    for d, frame in enumerate(frames):
        f_all[:, d * plan.pixels : (d + 1) * plan.pixels] = frame[...]
    taps[...] = mm(w_turned[: plan.cols, :], f_all[...], NN)
    total = None
    for tap, (distance, inside) in enumerate(shifts(plan, f_all.shape[1])):
        term = rolled(taps[tap * slab : (tap + 1) * slab, :], distance)
        term = jnp.where(inside, term, 0.0)
        total = term if total is None else total + term
    sigma = 1.0 / (1.0 + jnp.exp(-total))
    a_ref[...] = (total * sigma).astype(BF16)
    d_ref[...] = sigma * (1.0 + total * (1.0 - sigma))


def act_grads(plan, before_ref, own_ref, after_ref, wt_ref, send_ref, mine_ref, core_ref, total):
    low, _, _ = plan.place()
    slab = plan.slab
    here = mm(wt_ref[0], after_ref[...], NN)
    here = here + mm(wt_ref[1], own_ref[...], NN)
    here = here + mm(wt_ref[2], before_ref[...], NN)
    total[...] = here.astype(BF16)
    for d, ref in enumerate((mine_ref, core_ref)):
        place = slice(d * slab, (d + 1) * slab)
        ref[...] = total[pl.ds(pl.multiple_of((low ^ d) * slab, 16), slab), :]
        send_ref[place, :] = total[pl.ds(pl.multiple_of((low ^ (d + 2)) * slab, 16), slab), :]


def temporal(plan, a_ref, *refs):
    group, pixels, chans = plan.group, plan.pixels, plan.chans
    here_refs, halo_refs = refs[:group], refs[group : 2 * group]
    send_ref, keep_ref, total = refs[2 * group :]
    _, high, _ = plan.place()
    acts = a_ref[...]
    after = [ref[chans:, :] for ref in halo_refs]
    before = [ref[:chans, :] for ref in halo_refs]
    parts = []
    for grads in (after, [ref[...] for ref in here_refs], before):
        term = None
        for d in range(group):
            here = mm(grads[d], acts[:, d * pixels : (d + 1) * pixels], NT)
            term = here if term is None else term + here
        parts.append(term)
    if plan.tcols > 3 * plan.slab:
        parts.append(jnp.zeros((chans, plan.tcols - 3 * plan.slab), F32))
    total[...] = jnp.concatenate(parts, axis=1)
    size = plan.thalf
    keep_ref[...] = total[pl.ds(pl.multiple_of(high * size, 16), size), :]
    send_ref[...] = total[pl.ds(pl.multiple_of((1 - high) * size, 16), size), :].astype(BF16)


def spatial(plan, w_all, f_all, d_ref, mine_ref, core_ref, pair_ref, last_ref, *refs):
    s_send, s_keep, f_send, f_keep, expanded, total = refs
    _, high, _ = plan.place()
    pixels, slab, chans = plan.pixels, plan.slab, plan.chans
    parts = [mine_ref[...], core_ref[...], pair_ref[:slab, :], last_ref[...]]
    parts = [part.astype(F32) for part in parts]
    act_grad = jnp.concatenate(parts, axis=1)
    pre_grad = (act_grad * d_ref[...]).astype(BF16).astype(F32)
    moves = shifts(plan, pre_grad.shape[1])
    for tap, (distance, _) in enumerate(moves):
        inside = moves[8 - tap][1]
        term = jnp.where(inside, rolled(pre_grad, -distance), 0.0)
        expanded[tap * slab : (tap + 1) * slab, :] = term.astype(BF16)
    total[:, : plan.cols] = mm(f_all[...], expanded[...], NT)
    if plan.cols < total.shape[1]:
        total[:, plan.cols :] = jnp.zeros((chans, total.shape[1] - plan.cols), F32)
    size = plan.half
    s_keep[...] = total[:, pl.ds(pl.multiple_of(high * size, LANES), size)]
    s_send[...] = total[:, pl.ds(pl.multiple_of((1 - high) * size, LANES), size)].astype(BF16)
    grads = mm(w_all[:, : plan.cols], expanded[...], NN)
    for index in range(2):
        d = 2 * index
        here = slice(index * chans, (index + 1) * chans)
        f_keep[here, :] = grads[:, d * pixels : (d + 1) * pixels]
        f_send[here, :] = grads[:, (d + 1) * pixels : (d + 2) * pixels].astype(BF16)


def added(keep_ref, got_ref, own_ref, send_ref):
    total = keep_ref[...] + got_ref[...].astype(F32)
    own_ref[...] = total
    send_ref[...] = total.astype(BF16)


def space_halves(plan, keep_ref, got_ref, own_ref, send_ref, total):
    _, _, z = plan.place()
    rows = plan.rows
    total[...] = keep_ref[...] + got_ref[...].astype(F32)
    for n in range(2):
        place = slice(n * rows, (n + 1) * rows)
        own_ref[place, :] = total[pl.ds(pl.multiple_of((z ^ (2 * n)) * rows, 16), rows), :]
        send_ref[place, :] = total[pl.ds(pl.multiple_of((z ^ (2 * n + 1)) * rows, 16), rows), :].astype(BF16)


def space_quarter(plan, keep_ref, got_ref, own_ref, send_ref):
    rows = plan.rows
    own_ref[...] = keep_ref[:rows, :] + got_ref[:rows, :].astype(F32)
    send_ref[...] = (keep_ref[rows:, :] + got_ref[rows:, :].astype(F32)).astype(BF16)


def summed(own_ref, *refs):
    total = own_ref[...]
    for ref in refs[:-1]:
        total = total + ref[...].astype(F32)
    refs[-1][...] = total.astype(BF16)


def stacked(*refs):
    out_ref, first = refs[-1], 0
    for ref in refs[:-1]:
        out_ref[first : first + ref.shape[0], :] = ref[...]
        first += ref.shape[0]


def frame_half(plan, keep_ref, got_ref, send_ref, own_ref):
    chans = plan.chans
    own_ref[...] = keep_ref[:chans, :] + got_ref[:chans, :].astype(F32)
    send_ref[...] = (keep_ref[chans:, :] + got_ref[chans:, :].astype(F32)).astype(BF16)


def ends(t_own, t_got, *refs):
    chips, (t_sum, s_all) = refs[:4], refs[4:]
    summed(t_own, t_got, t_sum)
    stacked(*chips, s_all)


def space_end(plan, here_ref, core_ref, f_own, f_got, g_ref, out_ref, f_out, token_ref, held):
    low, high, _ = plan.place()
    group, slab, rows = plan.group, plan.slab, plan.rows
    for core, ref in enumerate((here_ref, core_ref)):
        for chip in range(4):
            other = high if chip < 2 else 1 - high
            lane = pl.multiple_of(other * plan.half, LANES)
            piece = ref[chip * rows : (chip + 1) * rows, :].astype(F32) * plan.factor
            held[low ^ (2 * (chip % 2) + core), :, pl.ds(lane, plan.half)] = piece
    for tap in range(9):
        out_ref[tap] = jnp.concatenate(
            [held[index, :, tap * slab : (tap + 1) * slab] for index in range(group)], axis=1
        )
    frame = f_own[...] + f_got[...].astype(F32)
    f_out[...] = (g_ref[...].astype(F32) + frame.T).astype(BF16)
    token_ref[...] = jnp.zeros_like(token_ref)


def time_end(plan, here_ref, core_ref, out_ref, held):
    low, high, _ = plan.place()
    slab, size = plan.slab, plan.thalf
    near = pl.ds(pl.multiple_of(high * size, 16), size)
    far = pl.ds(pl.multiple_of((1 - high) * size, 16), size)
    for core, ref in enumerate((here_ref, core_ref)):
        for pair in range(2):
            held[near, :] = ref[pair * size : (pair + 1) * size, :].astype(F32)
            held[far, :] = ref[(2 + pair) * size : (3 + pair) * size, :].astype(F32)
            turned = held[...].T * plan.factor
            for k in range(3):
                here = pl.ds(pl.multiple_of((low ^ (2 * pair + core)) * slab, 16), slab)
                out_ref[k, here, :] = turned[k * slab : (k + 1) * slab, :]


def per_device(plan, frames, cotangent, w_space, w_time):
    pixels, chans, group, seqs = plan.pixels, plan.chans, plan.group, plan.seqs
    slab, rows, half = plan.slab, plan.rows, plan.half
    lanes = group * pixels
    part = lambda fn: functools.partial(fn, plan)

    def swap(value, distance):
        return lax.ppermute(value, "clip", [(i, i ^ distance) for i in range(plan.clips)])

    def trade(value, distance):
        return lax.ppermute(value, "seq", [(i, i ^ distance) for i in range(seqs)])

    def turn(value, k):
        return lax.ppermute(value, "seq", [(i, (i + k) % seqs) for i in range(seqs)])

    def neighbours(value):
        z = lax.axis_index("seq")
        found = []
        for first in range(2):
            other = {i: i for i in range(seqs)}
            for i in range(first, seqs - 1, 2):
                other[i], other[i + 1] = i + 1, i
            found.append(lax.ppermute(value, "seq", list(other.items())))
        low, high = jnp.where(z % 2 == 1, *found), jnp.where(z % 2 == 1, *found[::-1])
        zero = jnp.zeros_like(value)
        return jnp.where(z == 0, zero, low), jnp.where(z == seqs - 1, zero, high)

    def gathered(own, pair):
        return own, swap(own, 1), pair, swap(pair, 1)

    def chips(value):
        return value, swap(value, 2), swap(value, group), swap(value, group + 2)

    clip_f, clip_g = frames.reshape(pixels, chans), cotangent.reshape(pixels, chans)
    taps = jnp.transpose(w_space, (1, 0, 2))
    frame = (chans, pixels)
    outs = [(frame, BF16), (frame, BF16), ((rows, 2 * half), BF16), ((rows, half), BF16)]
    frame_f, frame_g, piece, half_piece = pl.pallas_call(
        part(prepare),
        out_shape=tuple(jax.ShapeDtypeStruct(shape, dtype) for shape, dtype in outs),
        in_specs=[pl.BlockSpec(memory_space=pl.ANY)] * 3,
        out_specs=(VMEM,) * len(outs),
        scratch_shapes=[
            pltpu.VMEM(clip_f.shape, BF16),
            pltpu.VMEM(clip_g.shape, BF16),
            pltpu.VMEM(taps.shape, BF16),
            pltpu.SemaphoreType.DMA((3,)),
        ],
        compiler_params=pltpu.CompilerParams(vmem_limit_bytes=55_900_000),
    )(clip_f, clip_g, taps)

    w_got = [turn(half_piece, k) for k in range(1, seqs)]
    w_other = swap(jnp.concatenate(w_got, axis=0), group)
    pair_f, pair_g = swap(frame_f, 2), swap(frame_g, 2)
    before, after = neighbours(frame_g)
    d_send, d_mine, d_core = call(
        part(act_grads),
        [((2 * slab, pixels), BF16), ((slab, pixels), BF16), ((slab, pixels), BF16)],
        before,
        frame_g,
        after,
        w_time,
        scratch=[pltpu.VMEM(frame, BF16)],
    )
    d_pair = swap(d_send, 2)
    w_all, w_turned = call(
        part(weights),
        [((chans, 2 * half), BF16), ((2 * half, chans), BF16)],
        piece,
        *w_got,
        w_other,
        after=[pair_g],
    )
    (halo,) = call(
        stacked, [((2 * chans, pixels), BF16)], before, after, after=[w_all, d_pair]
    )
    f_all, acts, slope = call(
        part(forward),
        [((chans, lanes), BF16), ((slab, lanes), BF16), ((slab, lanes), F32)],
        w_turned,
        *gathered(frame_f, pair_f),
        after=[d_pair],
        scratch=[pltpu.VMEM((plan.cols, lanes), F32)],
    )
    s_send, s_keep, f_send, f_keep = call(
        part(spatial),
        [
            ((chans, half), BF16),
            ((chans, half), F32),
            ((2 * chans, pixels), BF16),
            ((2 * chans, pixels), F32),
        ],
        w_all,
        f_all,
        slope,
        d_mine,
        swap(d_core, 1),
        d_pair,
        swap(d_pair[slab:], 1),
        scratch=[pltpu.VMEM((plan.cols, lanes), BF16), pltpu.VMEM((chans, 2 * half), F32)],
    )
    time = (plan.thalf, plan.tcols)
    t_send, t_keep = call(
        part(temporal),
        [(time, BF16), (time, F32)],
        acts,
        *gathered(frame_g, pair_g),
        *gathered(halo, swap(halo, 2)),
        scratch=[pltpu.VMEM((chans, plan.tcols), F32)],
    )

    f_half, f_own = call(
        part(frame_half), [(frame, BF16), (frame, F32)], f_keep, swap(f_send, 1)
    )
    f_other = swap(f_half, 2)
    t_own, t_part = call(added, [(time, F32), (time, BF16)], t_keep, swap(t_send, group))
    t_own, t_part2 = call(added, [(time, F32), (time, BF16)], t_own, trade(t_part, 1))
    t_got = trade(t_part2, 2)
    s_own, s_part = call(
        part(space_halves),
        [((2 * rows, half), F32), ((2 * rows, half), BF16)],
        s_keep,
        swap(s_send, group),
        scratch=[pltpu.VMEM((chans, half), F32)],
    )
    s_own, s_part = call(
        part(space_quarter),
        [((rows, half), F32), ((rows, half), BF16)],
        s_own,
        trade(s_part, 1),
        after=[t_part],
    )
    (s_sum,) = call(
        summed, [((rows, half), BF16)], s_own, trade(s_part, 2), after=[f_other]
    )
    t_sum, s_all = call(
        ends, [(time, BF16), ((4 * rows, half), BF16)], t_own, t_got, *chips(s_sum)
    )
    s_out, f_out, token = call(
        part(space_end),
        [((9, rows, chans), F32), ((pixels, chans), BF16), ((8, LANES), F32)],
        s_all,
        swap(s_all, 1),
        f_own,
        f_other,
        clip_g,
        scratch=[pltpu.VMEM((group, rows, 2 * half), F32)],
    )
    (t_all,) = call(
        stacked, [((4 * plan.thalf, plan.tcols), BF16)], *chips(t_sum), after=[token]
    )
    (t_out,) = call(
        part(time_end),
        [((3, chans, chans), F32)],
        t_all,
        swap(t_all, 1),
        scratch=[pltpu.VMEM((chans, plan.tcols), F32)],
    )
    return f_out.reshape(frames.shape), jnp.transpose(s_out, (1, 0, 2)), t_out


def solution(mesh):
    in_specs = (
        P("clip", "seq", None, None, None),
        P("clip", "seq", None, None, None),
        P("seq", None, None),
        P(),
    )
    out_specs = (P("clip", "seq", None, None, None), P("seq", None, None), P())

    def body(frames, cotangent, w_space, w_time):
        one, count, height, width, chans = frames.shape
        plan = Plan(mesh.shape["clip"], mesh.shape["seq"], height, width, chans)
        if one == 1 and count == 1 and plan.fits():
            return per_device(plan, frames, cotangent, w_space, w_time)
        return per_device_general(frames, cotangent, w_space, w_time)

    return jax.shard_map(body, mesh=mesh, in_specs=in_specs, out_specs=out_specs, check_vma=False)
```

```python
import functools
import math

import jax
import jax.numpy as jnp
from jax import lax
from jax.experimental import pallas as pl
from jax.experimental.pallas import tpu as pltpu
from jax.sharding import PartitionSpec as P


def padded_2(cells, sides, width):
    for axis, dim in sides:
        count = lax.axis_size(axis)
        ends = count - 1
        head = lax.slice_in_dim(cells, 0, width, axis=dim)
        tail = lax.slice_in_dim(cells, cells.shape[dim] - width, cells.shape[dim], axis=dim)
        cells = jnp.concatenate(
            [
                lax.ppermute(tail, axis, [(i, (i + 1) % count) for i in range(ends)]),
                cells,
                lax.ppermute(head, axis, [((i + 1) % count, i) for i in range(ends)]),
            ],
            axis=dim,
        )
    return cells


def temporal_grads(acts, g_pad, w_time):
    count = acts.shape[0]
    chans = acts.shape[-1]
    flat_acts = acts.reshape(-1, chans)
    act_grad = jnp.zeros(flat_acts.shape, jnp.float32)
    time_terms = []
    for k in range(3):
        shifted = g_pad[2 - k : 2 - k + count].reshape(-1, chans)
        act_grad = act_grad + lax.dot_general(
            shifted, w_time[k], (((1,), (1,)), ((), ())), preferred_element_type=jnp.float32
        )
        time_terms.append(
            lax.dot_general(
                flat_acts, shifted, (((0,), (0,)), ((), ())), preferred_element_type=jnp.float32
            )
        )
    return (act_grad.astype(jnp.bfloat16).reshape(acts.shape), jnp.stack(time_terms, axis=0))


def per_device_general(frames, cotangent, w_space, w_time):
    weights = lax.all_gather(w_space, "seq", axis=0, tiled=True)
    clip_x = frames[0]
    clip_g = cotangent[0]
    count, height, width, chans = clip_x.shape
    factor = 1.0 / math.sqrt(lax.axis_size("clip") * count * lax.axis_size("seq") * height * width)
    padded = jnp.pad(clip_x, ((0, 0), (1, 1), (1, 1), (0, 0)))
    pieces = [
        padded[:, i : i + height, j : j + width, :].reshape(-1, chans)
        for i in range(3)
        for j in range(3)
    ]
    pre_act = jnp.zeros((count * height * width, chans), jnp.float32)
    for tap in range(9):
        pre_act = pre_act + jnp.dot(
            pieces[tap], weights[:, tap, :], preferred_element_type=jnp.float32
        )
    acts = jax.nn.silu(pre_act).astype(jnp.bfloat16).reshape(1, count, height, width, chans)
    g_rims = padded_2(cotangent, (("seq", 1),), 1)
    g_pad = g_rims[0].reshape(count + 2, height * width, chans)
    act_grad, time_terms = temporal_grads(
        acts[0].reshape(count, height * width, chans), g_pad, w_time
    )
    sigma = jax.nn.sigmoid(pre_act)
    pre_grad = (
        act_grad.reshape(-1, chans).astype(jnp.float32) * sigma * (1.0 + pre_act * (1.0 - sigma))
    ).astype(jnp.bfloat16)
    terms = []
    for tap in range(9):
        part = pieces[tap]
        terms.append(
            lax.dot_general(
                part, pre_grad, (((0,), (0,)), ((), ())), preferred_element_type=jnp.float32
            )
        )
    space_share = lax.psum_scatter(
        jnp.stack(terms, axis=1) * factor, "seq", scatter_dimension=0, tiled=True
    )
    space_grad = lax.psum(space_share, "clip")
    time_grad = lax.psum(time_terms * factor, ("clip", "seq"))
    grad_pad = jnp.pad(
        pre_grad.reshape(count, height, width, chans), ((0, 0), (1, 1), (1, 1), (0, 0))
    )
    input_grad = clip_g.reshape(-1, chans).astype(jnp.float32)
    for i in range(3):
        for j in range(3):
            piece = grad_pad[:, 2 - i : 2 - i + height, 2 - j : 2 - j + width, :].reshape(-1, chans)
            input_grad = input_grad + lax.dot_general(
                piece,
                weights[:, 3 * i + j, :],
                (((1,), (1,)), ((), ())),
                preferred_element_type=jnp.float32,
            )
    frames_grad = input_grad.astype(jnp.bfloat16).reshape(1, count, height, width, chans)
    return (frames_grad, space_grad, time_grad)


BF16 = jnp.bfloat16
F32 = jnp.float32
LANES = 128
VMEM = pl.BlockSpec(memory_space=pltpu.VMEM)
NN = (((1,), (0,)), ((), ()))
NT = (((1,), (1,)), ((), ()))
TN = (((0,), (0,)), ((), ()))


def round_up(value, unit):
    return -(-value // unit) * unit


def mm(lhs, rhs, dims):
    return lax.dot_general(lhs, rhs, dims, preferred_element_type=F32)


def call(kernel, outs, *args, after=(), scratch=()):
    def body(*refs):
        kernel(*refs[: len(args)], *refs[len(args) + len(after) :])

    return pl.pallas_call(
        body,
        out_shape=tuple(jax.ShapeDtypeStruct(shape, dtype) for shape, dtype in outs),
        in_specs=[VMEM] * len(args) + [pl.BlockSpec(memory_space=pl.ANY)] * len(after),
        out_specs=(VMEM,) * len(outs),
        scratch_shapes=list(scratch),
        compiler_params=pltpu.CompilerParams(vmem_limit_bytes=48 * 1024 * 1024),
    )(*args, *after)


class Plan:
    def __init__(self, clips, seqs, height, width, chans):
        self.clips, self.seqs = clips, seqs
        self.height, self.width, self.chans = height, width, chans
        self.group = clips // 2
        self.slab = chans // max(self.group, 1)
        self.rows = chans // seqs
        self.pixels = height * width
        self.cols = 9 * self.slab
        self.half = round_up(round_up(self.cols, 2 * LANES) // 2, LANES)
        self.tcols = round_up(3 * self.slab, LANES)
        self.thalf = chans // 2
        self.factor = 1.0 / math.sqrt(clips * seqs * self.pixels)

    def fits(self):
        return (
            self.group == 4
            and self.slab * self.group == self.chans
            and self.rows * self.seqs == self.chans
            and self.slab % 16 == 0
            and self.rows % 16 == 0
            and self.thalf % 16 == 0
            and self.pixels % LANES == 0
            and self.seqs == 4
        )

    def place(self):
        clip = lax.axis_index("clip")
        return clip % self.group, clip // self.group, lax.axis_index("seq")


def prepare(plan, f_hbm, g_hbm, w_hbm, ft_ref, gt_ref, wp_ref, wh_ref, f_ref, g_ref, w_ref, sems):
    low, high, _ = plan.place()
    slab, half = plan.slab, plan.half
    copies = [
        pltpu.make_async_copy(src, dst, sems.at[index])
        for index, (src, dst) in enumerate(((g_hbm, g_ref), (w_hbm, w_ref), (f_hbm, f_ref)))
    ]
    for copy in copies:
        copy.start()
    copies[0].wait()
    gt_ref[...] = g_ref[...].T
    copies[1].wait()
    for index in range(plan.group):

        @pl.when(low == index)
        def _():
            taps = [w_ref[tap][:, slab * index : slab * (index + 1)] for tap in range(9)]
            if plan.cols < 2 * half:
                taps.append(jnp.zeros((plan.rows, 2 * half - plan.cols), BF16))
            wp_ref[...] = jnp.concatenate(taps, axis=1)

    wh_ref[...] = wp_ref[:, pl.ds(pl.multiple_of(high * half, LANES), half)]
    copies[2].wait()
    ft_ref[...] = f_ref[...].T


def shifts(plan, lanes):
    lane = lax.broadcasted_iota(jnp.int32, (1, lanes), 1) % plan.pixels
    row, col = lane // plan.width, lane % plan.width
    found = []
    for i in range(3):
        for j in range(3):
            inside = (
                (row + (i - 1) >= 0)
                & (row + (i - 1) < plan.height)
                & (col + (j - 1) >= 0)
                & (col + (j - 1) < plan.width)
            )
            found.append(((i - 1) * plan.width + (j - 1), inside))
    return found


def rolled(value, distance):
    lanes = value.shape[1]
    return value if distance == 0 else pltpu.roll(value, (-distance) % lanes, 1)


def weights(plan, *refs):
    own_ref, got_refs, other_ref = refs[0], refs[1 : plan.seqs], refs[plan.seqs]
    w_all, w_turned = refs[plan.seqs + 1 :]
    _, high, z = plan.place()
    rows, half = plan.rows, plan.half
    here = pl.ds(pl.multiple_of(high * half, LANES), half)
    there = pl.ds(pl.multiple_of((1 - high) * half, LANES), half)
    w_all[pl.ds(pl.multiple_of(z * rows, 16), rows), :] = own_ref[...]
    for k, got_ref in enumerate(got_refs, 1):
        place = pl.ds(pl.multiple_of((z - k + plan.seqs) % plan.seqs * rows, 16), rows)
        w_all[place, here] = got_ref[...]
        w_all[place, there] = other_ref[(k - 1) * rows : k * rows, :]
    w_turned[...] = w_all[...].T


def forward(plan, w_turned, *refs):
    slab = plan.slab
    frames, (f_all, a_ref, d_ref, taps) = refs[: plan.group], refs[plan.group :]
    for d, frame in enumerate(frames):
        f_all[:, d * plan.pixels : (d + 1) * plan.pixels] = frame[...]
    taps[...] = mm(w_turned[: plan.cols, :], f_all[...], NN)
    total = None
    for tap, (distance, inside) in enumerate(shifts(plan, f_all.shape[1])):
        term = rolled(taps[tap * slab : (tap + 1) * slab, :], distance)
        term = jnp.where(inside, term, 0.0)
        total = term if total is None else total + term
    sigma = 1.0 / (1.0 + jnp.exp(-total))
    a_ref[...] = (total * sigma).astype(BF16)
    d_ref[...] = sigma * (1.0 + total * (1.0 - sigma))


def act_grads(plan, before_ref, own_ref, after_ref, wt_ref, send_ref, mine_ref, core_ref, total):
    low, _, _ = plan.place()
    slab = plan.slab
    here = mm(wt_ref[0], after_ref[...], NN)
    here = here + mm(wt_ref[1], own_ref[...], NN)
    here = here + mm(wt_ref[2], before_ref[...], NN)
    total[...] = here.astype(BF16)
    for d, ref in enumerate((mine_ref, core_ref)):
        place = slice(d * slab, (d + 1) * slab)
        ref[...] = total[pl.ds(pl.multiple_of((low ^ d) * slab, 16), slab), :]
        send_ref[place, :] = total[pl.ds(pl.multiple_of((low ^ (d + 2)) * slab, 16), slab), :]


def temporal(plan, a_ref, *refs):
    group, pixels, chans = plan.group, plan.pixels, plan.chans
    here_refs, halo_refs = refs[:group], refs[group : 2 * group]
    send_ref, keep_ref, total = refs[2 * group :]
    _, high, _ = plan.place()
    acts = a_ref[...]
    after = [ref[chans:, :] for ref in halo_refs]
    before = [ref[:chans, :] for ref in halo_refs]
    parts = []
    for grads in (after, [ref[...] for ref in here_refs], before):
        term = None
        for d in range(group):
            here = mm(grads[d], acts[:, d * pixels : (d + 1) * pixels], NT)
            term = here if term is None else term + here
        parts.append(term)
    if plan.tcols > 3 * plan.slab:
        parts.append(jnp.zeros((chans, plan.tcols - 3 * plan.slab), F32))
    total[...] = jnp.concatenate(parts, axis=1)
    size = plan.thalf
    keep_ref[...] = total[pl.ds(pl.multiple_of(high * size, 16), size), :]
    send_ref[...] = total[pl.ds(pl.multiple_of((1 - high) * size, 16), size), :].astype(BF16)


def spatial(plan, w_all, f_all, d_ref, mine_ref, core_ref, pair_ref, last_ref, *refs):
    s_send, s_keep, f_send, f_keep, expanded, total = refs
    _, high, _ = plan.place()
    pixels, slab, chans = plan.pixels, plan.slab, plan.chans
    parts = [mine_ref[...], core_ref[...], pair_ref[:slab, :], last_ref[...]]
    parts = [part.astype(F32) for part in parts]
    act_grad = jnp.concatenate(parts, axis=1)
    pre_grad = (act_grad * d_ref[...]).astype(BF16).astype(F32)
    moves = shifts(plan, pre_grad.shape[1])
    for tap, (distance, _) in enumerate(moves):
        inside = moves[8 - tap][1]
        term = jnp.where(inside, rolled(pre_grad, -distance), 0.0)
        expanded[tap * slab : (tap + 1) * slab, :] = term.astype(BF16)
    total[:, : plan.cols] = mm(f_all[...], expanded[...], NT)
    if plan.cols < total.shape[1]:
        total[:, plan.cols :] = jnp.zeros((chans, total.shape[1] - plan.cols), F32)
    size = plan.half
    s_keep[...] = total[:, pl.ds(pl.multiple_of(high * size, LANES), size)]
    s_send[...] = total[:, pl.ds(pl.multiple_of((1 - high) * size, LANES), size)].astype(BF16)
    grads = mm(w_all[:, : plan.cols], expanded[...], NN)
    for index in range(2):
        d = 2 * index
        here = slice(index * chans, (index + 1) * chans)
        f_keep[here, :] = grads[:, d * pixels : (d + 1) * pixels]
        f_send[here, :] = grads[:, (d + 1) * pixels : (d + 2) * pixels].astype(BF16)


def added(keep_ref, got_ref, own_ref, send_ref):
    total = keep_ref[...] + got_ref[...].astype(F32)
    own_ref[...] = total
    send_ref[...] = total.astype(BF16)


def space_halves(plan, keep_ref, got_ref, own_ref, send_ref, total):
    _, _, z = plan.place()
    rows = plan.rows
    total[...] = keep_ref[...] + got_ref[...].astype(F32)
    for n in range(2):
        place = slice(n * rows, (n + 1) * rows)
        own_ref[place, :] = total[pl.ds(pl.multiple_of((z ^ (2 * n)) * rows, 16), rows), :]
        send_ref[place, :] = total[pl.ds(pl.multiple_of((z ^ (2 * n + 1)) * rows, 16), rows), :].astype(BF16)


def space_quarter(plan, keep_ref, got_ref, own_ref, send_ref):
    rows = plan.rows
    own_ref[...] = keep_ref[:rows, :] + got_ref[:rows, :].astype(F32)
    send_ref[...] = (keep_ref[rows:, :] + got_ref[rows:, :].astype(F32)).astype(BF16)


def summed(own_ref, *refs):
    total = own_ref[...]
    for ref in refs[:-1]:
        total = total + ref[...].astype(F32)
    refs[-1][...] = total.astype(BF16)


def stacked(*refs):
    out_ref, first = refs[-1], 0
    for ref in refs[:-1]:
        out_ref[first : first + ref.shape[0], :] = ref[...]
        first += ref.shape[0]


def frame_half(plan, keep_ref, got_ref, send_ref, own_ref):
    chans = plan.chans
    own_ref[...] = keep_ref[:chans, :] + got_ref[:chans, :].astype(F32)
    send_ref[...] = (keep_ref[chans:, :] + got_ref[chans:, :].astype(F32)).astype(BF16)


def ends(t_own, t_got, *refs):
    chips, (t_sum, s_all) = refs[:4], refs[4:]
    summed(t_own, t_got, t_sum)
    stacked(*chips, s_all)


def space_end(plan, here_ref, core_ref, f_own, f_got, g_ref, out_ref, f_out, token_ref, held):
    low, high, _ = plan.place()
    group, slab, rows = plan.group, plan.slab, plan.rows
    for core, ref in enumerate((here_ref, core_ref)):
        for chip in range(4):
            other = high if chip < 2 else 1 - high
            lane = pl.multiple_of(other * plan.half, LANES)
            piece = ref[chip * rows : (chip + 1) * rows, :].astype(F32) * plan.factor
            held[low ^ (2 * (chip % 2) + core), :, pl.ds(lane, plan.half)] = piece
    for tap in range(9):
        out_ref[tap] = jnp.concatenate(
            [held[index, :, tap * slab : (tap + 1) * slab] for index in range(group)], axis=1
        )
    frame = f_own[...] + f_got[...].astype(F32)
    f_out[...] = (g_ref[...].astype(F32) + frame.T).astype(BF16)
    token_ref[...] = jnp.zeros_like(token_ref)


def time_end(plan, here_ref, core_ref, out_ref, held):
    low, high, _ = plan.place()
    slab, size = plan.slab, plan.thalf
    near = pl.ds(pl.multiple_of(high * size, 16), size)
    far = pl.ds(pl.multiple_of((1 - high) * size, 16), size)
    for core, ref in enumerate((here_ref, core_ref)):
        for pair in range(2):
            held[near, :] = ref[pair * size : (pair + 1) * size, :].astype(F32)
            held[far, :] = ref[(2 + pair) * size : (3 + pair) * size, :].astype(F32)
            turned = held[...].T * plan.factor
            for k in range(3):
                here = pl.ds(pl.multiple_of((low ^ (2 * pair + core)) * slab, 16), slab)
                out_ref[k, here, :] = turned[k * slab : (k + 1) * slab, :]


def per_device(plan, frames, cotangent, w_space, w_time):
    pixels, chans, group, seqs = plan.pixels, plan.chans, plan.group, plan.seqs
    slab, rows, half = plan.slab, plan.rows, plan.half
    lanes = group * pixels
    part = lambda fn: functools.partial(fn, plan)

    def swap(value, distance):
        return lax.ppermute(value, "clip", [(i, i ^ distance) for i in range(plan.clips)])

    def trade(value, distance):
        return lax.ppermute(value, "seq", [(i, i ^ distance) for i in range(seqs)])

    def turn(value, k):
        return lax.ppermute(value, "seq", [(i, (i + k) % seqs) for i in range(seqs)])

    def neighbours(value):
        z = lax.axis_index("seq")
        found = []
        for first in range(2):
            other = {i: i for i in range(seqs)}
            for i in range(first, seqs - 1, 2):
                other[i], other[i + 1] = i + 1, i
            found.append(lax.ppermute(value, "seq", list(other.items())))
        low, high = jnp.where(z % 2 == 1, *found), jnp.where(z % 2 == 1, *found[::-1])
        zero = jnp.zeros_like(value)
        return jnp.where(z == 0, zero, low), jnp.where(z == seqs - 1, zero, high)

    def gathered(own, pair):
        return own, swap(own, 1), pair, swap(pair, 1)

    def chips(value):
        return value, swap(value, 2), swap(value, group), swap(value, group + 2)

    clip_f, clip_g = frames.reshape(pixels, chans), cotangent.reshape(pixels, chans)
    taps = jnp.transpose(w_space, (1, 0, 2))
    frame = (chans, pixels)
    outs = [(frame, BF16), (frame, BF16), ((rows, 2 * half), BF16), ((rows, half), BF16)]
    frame_f, frame_g, piece, half_piece = pl.pallas_call(
        part(prepare),
        out_shape=tuple(jax.ShapeDtypeStruct(shape, dtype) for shape, dtype in outs),
        in_specs=[pl.BlockSpec(memory_space=pl.ANY)] * 3,
        out_specs=(VMEM,) * len(outs),
        scratch_shapes=[
            pltpu.VMEM(clip_f.shape, BF16),
            pltpu.VMEM(clip_g.shape, BF16),
            pltpu.VMEM(taps.shape, BF16),
            pltpu.SemaphoreType.DMA((3,)),
        ],
        compiler_params=pltpu.CompilerParams(vmem_limit_bytes=55_900_000),
    )(clip_f, clip_g, taps)

    w_got = [turn(half_piece, k) for k in range(1, seqs)]
    w_other = swap(jnp.concatenate(w_got, axis=0), group)
    pair_f, pair_g = swap(frame_f, 2), swap(frame_g, 2)
    before, after = neighbours(frame_g)
    d_send, d_mine, d_core = call(
        part(act_grads),
        [((2 * slab, pixels), BF16), ((slab, pixels), BF16), ((slab, pixels), BF16)],
        before,
        frame_g,
        after,
        w_time,
        scratch=[pltpu.VMEM(frame, BF16)],
    )
    d_pair = swap(d_send, 2)
    w_all, w_turned = call(
        part(weights),
        [((chans, 2 * half), BF16), ((2 * half, chans), BF16)],
        piece,
        *w_got,
        w_other,
        after=[pair_g],
    )
    f_all, acts, slope = call(
        part(forward),
        [((chans, lanes), BF16), ((slab, lanes), BF16), ((slab, lanes), F32)],
        w_turned,
        *gathered(frame_f, pair_f),
        scratch=[pltpu.VMEM((plan.cols, lanes), F32)],
    )
    d_core, d_last = swap(d_core, 1), swap(d_pair[slab:], 1)
    (halo,) = call(
        stacked,
        [((2 * chans, pixels), BF16)],
        before,
        after,
        after=[w_all, d_pair, d_core, f_all],
    )
    s_send, s_keep, f_send, f_keep = call(
        part(spatial),
        [
            ((chans, half), BF16),
            ((chans, half), F32),
            ((2 * chans, pixels), BF16),
            ((2 * chans, pixels), F32),
        ],
        w_all,
        f_all,
        slope,
        d_mine,
        d_core,
        d_pair,
        d_last,
        scratch=[pltpu.VMEM((plan.cols, lanes), BF16), pltpu.VMEM((chans, 2 * half), F32)],
    )
    time = (plan.thalf, plan.tcols)
    t_send, t_keep = call(
        part(temporal),
        [(time, BF16), (time, F32)],
        acts,
        *gathered(frame_g, pair_g),
        *gathered(halo, swap(halo, 2)),
        scratch=[pltpu.VMEM((chans, plan.tcols), F32)],
    )

    f_half, f_own = call(
        part(frame_half), [(frame, BF16), (frame, F32)], f_keep, swap(f_send, 1)
    )
    f_other = swap(f_half, 2)
    s_own, s_part = call(
        part(space_halves),
        [((2 * rows, half), F32), ((2 * rows, half), BF16)],
        s_keep,
        swap(s_send, group),
        scratch=[pltpu.VMEM((chans, half), F32)],
    )
    s_own, s_part = call(
        part(space_quarter),
        [((rows, half), F32), ((rows, half), BF16)],
        s_own,
        trade(s_part, 1),
    )
    t_own, t_part = call(
        added, [(time, F32), (time, BF16)], t_keep, swap(t_send, group), after=[s_own]
    )
    t_own, t_part = call(added, [(time, F32), (time, BF16)], t_own, trade(t_part, 1))
    t_got = trade(t_part, 2)
    (s_sum,) = call(
        summed, [((rows, half), BF16)], s_own, trade(s_part, 2), after=[f_other]
    )
    t_sum, s_all = call(
        ends, [(time, BF16), ((4 * rows, half), BF16)], t_own, t_got, *chips(s_sum)
    )
    s_out, f_out, token = call(
        part(space_end),
        [((9, rows, chans), F32), ((pixels, chans), BF16), ((8, LANES), F32)],
        s_all,
        swap(s_all, 1),
        f_own,
        f_other,
        clip_g,
        scratch=[pltpu.VMEM((group, rows, 2 * half), F32)],
    )
    (t_all,) = call(
        stacked, [((4 * plan.thalf, plan.tcols), BF16)], *chips(t_sum), after=[token]
    )
    (t_out,) = call(
        part(time_end),
        [((3, chans, chans), F32)],
        t_all,
        swap(t_all, 1),
        scratch=[pltpu.VMEM((chans, plan.tcols), F32)],
    )
    return f_out.reshape(frames.shape), jnp.transpose(s_out, (1, 0, 2)), t_out


def solution(mesh):
    in_specs = (
        P("clip", "seq", None, None, None),
        P("clip", "seq", None, None, None),
        P("seq", None, None),
        P(),
    )
    out_specs = (P("clip", "seq", None, None, None), P("seq", None, None), P())

    def body(frames, cotangent, w_space, w_time):
        one, count, height, width, chans = frames.shape
        plan = Plan(mesh.shape["clip"], mesh.shape["seq"], height, width, chans)
        if one == 1 and count == 1 and plan.fits():
            return per_device(plan, frames, cotangent, w_space, w_time)
        return per_device_general(frames, cotangent, w_space, w_time)

    return jax.shard_map(body, mesh=mesh, in_specs=in_specs, out_specs=out_specs, check_vma=False)
```

```python
import functools
import math

import jax
import jax.numpy as jnp
from jax import lax
from jax.experimental import pallas as pl
from jax.experimental.pallas import tpu as pltpu
from jax.sharding import PartitionSpec as P


def padded_2(cells, sides, width):
    for axis, dim in sides:
        count = lax.axis_size(axis)
        ends = count - 1
        head = lax.slice_in_dim(cells, 0, width, axis=dim)
        tail = lax.slice_in_dim(cells, cells.shape[dim] - width, cells.shape[dim], axis=dim)
        cells = jnp.concatenate(
            [
                lax.ppermute(tail, axis, [(i, (i + 1) % count) for i in range(ends)]),
                cells,
                lax.ppermute(head, axis, [((i + 1) % count, i) for i in range(ends)]),
            ],
            axis=dim,
        )
    return cells


def temporal_grads(acts, g_pad, w_time):
    count = acts.shape[0]
    chans = acts.shape[-1]
    flat_acts = acts.reshape(-1, chans)
    act_grad = jnp.zeros(flat_acts.shape, jnp.float32)
    time_terms = []
    for k in range(3):
        shifted = g_pad[2 - k : 2 - k + count].reshape(-1, chans)
        act_grad = act_grad + lax.dot_general(
            shifted, w_time[k], (((1,), (1,)), ((), ())), preferred_element_type=jnp.float32
        )
        time_terms.append(
            lax.dot_general(
                flat_acts, shifted, (((0,), (0,)), ((), ())), preferred_element_type=jnp.float32
            )
        )
    return (act_grad.astype(jnp.bfloat16).reshape(acts.shape), jnp.stack(time_terms, axis=0))


def per_device_general(frames, cotangent, w_space, w_time):
    weights = lax.all_gather(w_space, "seq", axis=0, tiled=True)
    clip_x = frames[0]
    clip_g = cotangent[0]
    count, height, width, chans = clip_x.shape
    factor = 1.0 / math.sqrt(lax.axis_size("clip") * count * lax.axis_size("seq") * height * width)
    padded = jnp.pad(clip_x, ((0, 0), (1, 1), (1, 1), (0, 0)))
    pieces = [
        padded[:, i : i + height, j : j + width, :].reshape(-1, chans)
        for i in range(3)
        for j in range(3)
    ]
    pre_act = jnp.zeros((count * height * width, chans), jnp.float32)
    for tap in range(9):
        pre_act = pre_act + jnp.dot(
            pieces[tap], weights[:, tap, :], preferred_element_type=jnp.float32
        )
    acts = jax.nn.silu(pre_act).astype(jnp.bfloat16).reshape(1, count, height, width, chans)
    g_rims = padded_2(cotangent, (("seq", 1),), 1)
    g_pad = g_rims[0].reshape(count + 2, height * width, chans)
    act_grad, time_terms = temporal_grads(
        acts[0].reshape(count, height * width, chans), g_pad, w_time
    )
    sigma = jax.nn.sigmoid(pre_act)
    pre_grad = (
        act_grad.reshape(-1, chans).astype(jnp.float32) * sigma * (1.0 + pre_act * (1.0 - sigma))
    ).astype(jnp.bfloat16)
    terms = []
    for tap in range(9):
        part = pieces[tap]
        terms.append(
            lax.dot_general(
                part, pre_grad, (((0,), (0,)), ((), ())), preferred_element_type=jnp.float32
            )
        )
    space_share = lax.psum_scatter(
        jnp.stack(terms, axis=1) * factor, "seq", scatter_dimension=0, tiled=True
    )
    space_grad = lax.psum(space_share, "clip")
    time_grad = lax.psum(time_terms * factor, ("clip", "seq"))
    grad_pad = jnp.pad(
        pre_grad.reshape(count, height, width, chans), ((0, 0), (1, 1), (1, 1), (0, 0))
    )
    input_grad = clip_g.reshape(-1, chans).astype(jnp.float32)
    for i in range(3):
        for j in range(3):
            piece = grad_pad[:, 2 - i : 2 - i + height, 2 - j : 2 - j + width, :].reshape(-1, chans)
            input_grad = input_grad + lax.dot_general(
                piece,
                weights[:, 3 * i + j, :],
                (((1,), (1,)), ((), ())),
                preferred_element_type=jnp.float32,
            )
    frames_grad = input_grad.astype(jnp.bfloat16).reshape(1, count, height, width, chans)
    return (frames_grad, space_grad, time_grad)


BF16 = jnp.bfloat16
F32 = jnp.float32
LANES = 128
VMEM = pl.BlockSpec(memory_space=pltpu.VMEM)
NN = (((1,), (0,)), ((), ()))
NT = (((1,), (1,)), ((), ()))
TN = (((0,), (0,)), ((), ()))


def round_up(value, unit):
    return -(-value // unit) * unit


def mm(lhs, rhs, dims):
    return lax.dot_general(lhs, rhs, dims, preferred_element_type=F32)


def call(kernel, outs, *args, after=(), scratch=()):
    def body(*refs):
        kernel(*refs[: len(args)], *refs[len(args) + len(after) :])

    return pl.pallas_call(
        body,
        out_shape=tuple(jax.ShapeDtypeStruct(shape, dtype) for shape, dtype in outs),
        in_specs=[VMEM] * len(args) + [pl.BlockSpec(memory_space=pl.ANY)] * len(after),
        out_specs=(VMEM,) * len(outs),
        scratch_shapes=list(scratch),
        compiler_params=pltpu.CompilerParams(vmem_limit_bytes=48 * 1024 * 1024),
    )(*args, *after)


class Plan:
    def __init__(self, clips, seqs, height, width, chans):
        self.clips, self.seqs = clips, seqs
        self.height, self.width, self.chans = height, width, chans
        self.group = clips // 2
        self.slab = chans // max(self.group, 1)
        self.rows = chans // seqs
        self.pixels = height * width
        self.cols = 9 * self.slab
        self.half = round_up(round_up(self.cols, 2 * LANES) // 2, LANES)
        self.tcols = round_up(3 * self.slab, LANES)
        self.thalf = chans // 2
        self.chips = (0, self.group + 2, self.group, 2)
        self.factor = 1.0 / math.sqrt(clips * seqs * self.pixels)

    def fits(self):
        return (
            self.group == 4
            and self.slab * self.group == self.chans
            and self.rows * self.seqs == self.chans
            and self.slab % 16 == 0
            and self.rows % 16 == 0
            and self.thalf % 16 == 0
            and self.pixels % LANES == 0
            and self.seqs == 4
        )

    def place(self):
        clip = lax.axis_index("clip")
        return clip % self.group, clip // self.group, lax.axis_index("seq")


def prepare(plan, f_hbm, g_hbm, w_hbm, ft_ref, gt_ref, wp_ref, wh_ref, f_ref, g_ref, w_ref, sems):
    low, high, _ = plan.place()
    slab, half = plan.slab, plan.half
    copies = [
        pltpu.make_async_copy(src, dst, sems.at[index])
        for index, (src, dst) in enumerate(((g_hbm, g_ref), (w_hbm, w_ref), (f_hbm, f_ref)))
    ]
    for copy in copies:
        copy.start()
    copies[0].wait()
    gt_ref[...] = g_ref[...].T
    copies[1].wait()
    for index in range(plan.group):

        @pl.when(low == index)
        def _():
            taps = [w_ref[tap][:, slab * index : slab * (index + 1)] for tap in range(9)]
            if plan.cols < 2 * half:
                taps.append(jnp.zeros((plan.rows, 2 * half - plan.cols), BF16))
            wp_ref[...] = jnp.concatenate(taps, axis=1)

    wh_ref[...] = wp_ref[:, pl.ds(pl.multiple_of(high * half, LANES), half)]
    copies[2].wait()
    ft_ref[...] = f_ref[...].T


def shifts(plan, lanes):
    lane = lax.broadcasted_iota(jnp.int32, (1, lanes), 1) % plan.pixels
    row, col = lane // plan.width, lane % plan.width
    found = []
    for i in range(3):
        for j in range(3):
            inside = (
                (row + (i - 1) >= 0)
                & (row + (i - 1) < plan.height)
                & (col + (j - 1) >= 0)
                & (col + (j - 1) < plan.width)
            )
            found.append(((i - 1) * plan.width + (j - 1), inside))
    return found


def rolled(value, distance):
    lanes = value.shape[1]
    return value if distance == 0 else pltpu.roll(value, (-distance) % lanes, 1)


def weights(plan, *refs):
    own_ref, got_refs, other_ref = refs[0], refs[1 : plan.seqs], refs[plan.seqs]
    w_all, w_turned = refs[plan.seqs + 1 :]
    _, high, z = plan.place()
    rows, half = plan.rows, plan.half
    here = pl.ds(pl.multiple_of(high * half, LANES), half)
    there = pl.ds(pl.multiple_of((1 - high) * half, LANES), half)
    w_all[pl.ds(pl.multiple_of(z * rows, 16), rows), :] = own_ref[...]
    for k, got_ref in enumerate(got_refs, 1):
        place = pl.ds(pl.multiple_of((z - k + plan.seqs) % plan.seqs * rows, 16), rows)
        w_all[place, here] = got_ref[...]
        w_all[place, there] = other_ref[(k - 1) * rows : k * rows, :]
    w_turned[...] = w_all[...].T


def forward(plan, w_turned, *refs):
    slab = plan.slab
    frames, (f_all, a_ref, d_ref, taps) = refs[: plan.group], refs[plan.group :]
    for d, frame in enumerate(frames):
        f_all[:, d * plan.pixels : (d + 1) * plan.pixels] = frame[...]
    taps[...] = mm(w_turned[: plan.cols, :], f_all[...], NN)
    total = None
    for tap, (distance, inside) in enumerate(shifts(plan, f_all.shape[1])):
        term = rolled(taps[tap * slab : (tap + 1) * slab, :], distance)
        term = jnp.where(inside, term, 0.0)
        total = term if total is None else total + term
    sigma = 1.0 / (1.0 + jnp.exp(-total))
    a_ref[...] = (total * sigma).astype(BF16)
    d_ref[...] = sigma * (1.0 + total * (1.0 - sigma))


def act_grads(plan, before_ref, own_ref, after_ref, wt_ref, send_ref, mine_ref, core_ref, total):
    low, _, _ = plan.place()
    slab = plan.slab
    here = mm(wt_ref[0], after_ref[...], NN)
    here = here + mm(wt_ref[1], own_ref[...], NN)
    here = here + mm(wt_ref[2], before_ref[...], NN)
    total[...] = here.astype(BF16)
    for d, ref in enumerate((mine_ref, core_ref)):
        place = slice(d * slab, (d + 1) * slab)
        ref[...] = total[pl.ds(pl.multiple_of((low ^ d) * slab, 16), slab), :]
        send_ref[place, :] = total[pl.ds(pl.multiple_of((low ^ (d + 2)) * slab, 16), slab), :]


def temporal(plan, a_ref, *refs):
    group, pixels, chans = plan.group, plan.pixels, plan.chans
    here_refs, halo_refs = refs[:group], refs[group : 2 * group]
    send_ref, keep_ref, total = refs[2 * group :]
    _, high, _ = plan.place()
    acts = a_ref[...]
    after = [ref[chans:, :] for ref in halo_refs]
    before = [ref[:chans, :] for ref in halo_refs]
    parts = []
    for grads in (after, [ref[...] for ref in here_refs], before):
        term = None
        for d in range(group):
            here = mm(grads[d], acts[:, d * pixels : (d + 1) * pixels], NT)
            term = here if term is None else term + here
        parts.append(term)
    if plan.tcols > 3 * plan.slab:
        parts.append(jnp.zeros((chans, plan.tcols - 3 * plan.slab), F32))
    total[...] = jnp.concatenate(parts, axis=1)
    size = plan.thalf
    keep_ref[...] = total[pl.ds(pl.multiple_of(high * size, 16), size), :]
    send_ref[...] = total[pl.ds(pl.multiple_of((1 - high) * size, 16), size), :].astype(BF16)


def spatial(plan, w_all, f_all, d_ref, mine_ref, core_ref, pair_ref, last_ref, *refs):
    s_send, s_keep, f_send, f_keep, expanded, total = refs
    _, high, _ = plan.place()
    pixels, slab, chans = plan.pixels, plan.slab, plan.chans
    parts = [mine_ref[...], core_ref[...], pair_ref[:slab, :], last_ref[...]]
    parts = [part.astype(F32) for part in parts]
    act_grad = jnp.concatenate(parts, axis=1)
    pre_grad = (act_grad * d_ref[...]).astype(BF16).astype(F32)
    moves = shifts(plan, pre_grad.shape[1])
    for tap, (distance, _) in enumerate(moves):
        inside = moves[8 - tap][1]
        term = jnp.where(inside, rolled(pre_grad, -distance), 0.0)
        expanded[tap * slab : (tap + 1) * slab, :] = term.astype(BF16)
    total[:, : plan.cols] = mm(f_all[...], expanded[...], NT)
    if plan.cols < total.shape[1]:
        total[:, plan.cols :] = jnp.zeros((chans, total.shape[1] - plan.cols), F32)
    size = plan.half
    s_keep[...] = total[:, pl.ds(pl.multiple_of(high * size, LANES), size)]
    s_send[...] = total[:, pl.ds(pl.multiple_of((1 - high) * size, LANES), size)].astype(BF16)
    grads = mm(w_all[:, : plan.cols], expanded[...], NN)
    for index in range(2):
        d = 2 * index
        here = slice(index * chans, (index + 1) * chans)
        f_keep[here, :] = grads[:, d * pixels : (d + 1) * pixels]
        f_send[here, :] = grads[:, (d + 1) * pixels : (d + 2) * pixels].astype(BF16)


def added(keep_ref, got_ref, own_ref, send_ref):
    total = keep_ref[...] + got_ref[...].astype(F32)
    own_ref[...] = total
    send_ref[...] = total.astype(BF16)


def space_halves(plan, keep_ref, got_ref, own_ref, send_ref, total):
    _, _, z = plan.place()
    rows = plan.rows
    total[...] = keep_ref[...] + got_ref[...].astype(F32)
    for n in range(2):
        place = slice(n * rows, (n + 1) * rows)
        own_ref[place, :] = total[pl.ds(pl.multiple_of((z ^ (2 * n)) * rows, 16), rows), :]
        send_ref[place, :] = total[pl.ds(pl.multiple_of((z ^ (2 * n + 1)) * rows, 16), rows), :].astype(BF16)


def space_quarter(plan, keep_ref, got_ref, own_ref, send_ref):
    rows = plan.rows
    own_ref[...] = keep_ref[:rows, :] + got_ref[:rows, :].astype(F32)
    send_ref[...] = (keep_ref[rows:, :] + got_ref[rows:, :].astype(F32)).astype(BF16)


def summed(own_ref, *refs):
    total = own_ref[...]
    for ref in refs[:-1]:
        total = total + ref[...].astype(F32)
    refs[-1][...] = total.astype(BF16)


def stacked(*refs):
    out_ref, first = refs[-1], 0
    for ref in refs[:-1]:
        out_ref[first : first + ref.shape[0], :] = ref[...]
        first += ref.shape[0]


def frame_half(plan, keep_ref, got_ref, send_ref, own_ref):
    chans = plan.chans
    own_ref[...] = keep_ref[:chans, :] + got_ref[:chans, :].astype(F32)
    send_ref[...] = (keep_ref[chans:, :] + got_ref[chans:, :].astype(F32)).astype(BF16)


def ends(t_own, t_got, *refs):
    chips, (t_sum, s_all) = refs[:4], refs[4:]
    summed(t_own, t_got, t_sum)
    stacked(*chips, s_all)


def space_end(plan, here_ref, core_ref, f_own, f_got, g_ref, out_ref, f_out, token_ref, held):
    low, high, _ = plan.place()
    group, slab, rows = plan.group, plan.slab, plan.rows
    for core, ref in enumerate((here_ref, core_ref)):
        for chip, distance in enumerate(plan.chips):
            other = high if distance < group else 1 - high
            lane = pl.multiple_of(other * plan.half, LANES)
            piece = ref[chip * rows : (chip + 1) * rows, :].astype(F32) * plan.factor
            held[low ^ (distance % group + core), :, pl.ds(lane, plan.half)] = piece
    for tap in range(9):
        out_ref[tap] = jnp.concatenate(
            [held[index, :, tap * slab : (tap + 1) * slab] for index in range(group)], axis=1
        )
    frame = f_own[...] + f_got[...].astype(F32)
    f_out[...] = (g_ref[...].astype(F32) + frame.T).astype(BF16)
    token_ref[...] = jnp.zeros_like(token_ref)


def time_end(plan, here_ref, core_ref, out_ref, held):
    low, high, _ = plan.place()
    slab, size = plan.slab, plan.thalf
    near = pl.ds(pl.multiple_of(high * size, 16), size)
    far = pl.ds(pl.multiple_of((1 - high) * size, 16), size)
    for core, ref in enumerate((here_ref, core_ref)):
        for pair in range(2):
            first = plan.chips.index(2 * pair) * size
            second = plan.chips.index(plan.group + 2 * pair) * size
            held[near, :] = ref[first : first + size, :].astype(F32)
            held[far, :] = ref[second : second + size, :].astype(F32)
            turned = held[...].T * plan.factor
            for k in range(3):
                here = pl.ds(pl.multiple_of((low ^ (2 * pair + core)) * slab, 16), slab)
                out_ref[k, here, :] = turned[k * slab : (k + 1) * slab, :]


def per_device(plan, frames, cotangent, w_space, w_time):
    pixels, chans, group, seqs = plan.pixels, plan.chans, plan.group, plan.seqs
    slab, rows, half = plan.slab, plan.rows, plan.half
    lanes = group * pixels
    part = lambda fn: functools.partial(fn, plan)

    def swap(value, distance):
        return lax.ppermute(value, "clip", [(i, i ^ distance) for i in range(plan.clips)])

    def trade(value, distance):
        return lax.ppermute(value, "seq", [(i, i ^ distance) for i in range(seqs)])

    def turn(value, k):
        return lax.ppermute(value, "seq", [(i, (i + k) % seqs) for i in range(seqs)])

    def neighbours(value):
        z = lax.axis_index("seq")
        found = []
        for first in range(2):
            other = {i: i for i in range(seqs)}
            for i in range(first, seqs - 1, 2):
                other[i], other[i + 1] = i + 1, i
            found.append(lax.ppermute(value, "seq", list(other.items())))
        low, high = jnp.where(z % 2 == 1, *found), jnp.where(z % 2 == 1, *found[::-1])
        zero = jnp.zeros_like(value)
        return jnp.where(z == 0, zero, low), jnp.where(z == seqs - 1, zero, high)

    def gathered(own, pair):
        return own, swap(own, 1), pair, swap(pair, 1)

    def chips(value):
        return (value, *(swap(value, distance) for distance in plan.chips[1:]))

    clip_f, clip_g = frames.reshape(pixels, chans), cotangent.reshape(pixels, chans)
    taps = jnp.transpose(w_space, (1, 0, 2))
    frame = (chans, pixels)
    outs = [(frame, BF16), (frame, BF16), ((rows, 2 * half), BF16), ((rows, half), BF16)]
    frame_f, frame_g, piece, half_piece = pl.pallas_call(
        part(prepare),
        out_shape=tuple(jax.ShapeDtypeStruct(shape, dtype) for shape, dtype in outs),
        in_specs=[pl.BlockSpec(memory_space=pl.ANY)] * 3,
        out_specs=(VMEM,) * len(outs),
        scratch_shapes=[
            pltpu.VMEM(clip_f.shape, BF16),
            pltpu.VMEM(clip_g.shape, BF16),
            pltpu.VMEM(taps.shape, BF16),
            pltpu.SemaphoreType.DMA((3,)),
        ],
        compiler_params=pltpu.CompilerParams(vmem_limit_bytes=55_900_000),
    )(clip_f, clip_g, taps)

    w_got = [turn(half_piece, k) for k in range(1, seqs)]
    w_other = swap(jnp.concatenate(w_got, axis=0), group)
    pair_f, pair_g = swap(frame_f, 2), swap(frame_g, 2)
    before, after = neighbours(frame_g)
    d_send, d_mine, d_core = call(
        part(act_grads),
        [((2 * slab, pixels), BF16), ((slab, pixels), BF16), ((slab, pixels), BF16)],
        before,
        frame_g,
        after,
        w_time,
        scratch=[pltpu.VMEM(frame, BF16)],
    )
    d_pair = swap(d_send, 2)
    w_all, w_turned = call(
        part(weights),
        [((chans, 2 * half), BF16), ((2 * half, chans), BF16)],
        piece,
        *w_got,
        w_other,
        after=[pair_g],
    )
    f_all, acts, slope = call(
        part(forward),
        [((chans, lanes), BF16), ((slab, lanes), BF16), ((slab, lanes), F32)],
        w_turned,
        *gathered(frame_f, pair_f),
        scratch=[pltpu.VMEM((plan.cols, lanes), F32)],
    )
    d_core, d_last = swap(d_core, 1), swap(d_pair[slab:], 1)
    (halo,) = call(
        stacked,
        [((2 * chans, pixels), BF16)],
        before,
        after,
        after=[w_all, d_pair, d_core, f_all],
    )
    s_send, s_keep, f_send, f_keep = call(
        part(spatial),
        [
            ((chans, half), BF16),
            ((chans, half), F32),
            ((2 * chans, pixels), BF16),
            ((2 * chans, pixels), F32),
        ],
        w_all,
        f_all,
        slope,
        d_mine,
        d_core,
        d_pair,
        d_last,
        scratch=[pltpu.VMEM((plan.cols, lanes), BF16), pltpu.VMEM((chans, 2 * half), F32)],
    )
    time = (plan.thalf, plan.tcols)
    t_send, t_keep = call(
        part(temporal),
        [(time, BF16), (time, F32)],
        acts,
        *gathered(frame_g, pair_g),
        *gathered(halo, swap(halo, 2)),
        scratch=[pltpu.VMEM((chans, plan.tcols), F32)],
    )

    f_half, f_own = call(
        part(frame_half), [(frame, BF16), (frame, F32)], f_keep, swap(f_send, 1)
    )
    f_other = swap(f_half, 2)
    s_own, s_part = call(
        part(space_halves),
        [((2 * rows, half), F32), ((2 * rows, half), BF16)],
        s_keep,
        swap(s_send, group),
        scratch=[pltpu.VMEM((chans, half), F32)],
    )
    s_own, s_part = call(
        part(space_quarter),
        [((rows, half), F32), ((rows, half), BF16)],
        s_own,
        trade(s_part, 1),
    )
    t_own, t_part = call(
        added, [(time, F32), (time, BF16)], t_keep, swap(t_send, group), after=[s_own]
    )
    t_own, t_part = call(added, [(time, F32), (time, BF16)], t_own, trade(t_part, 1))
    t_got = trade(t_part, 2)
    (s_sum,) = call(
        summed, [((rows, half), BF16)], s_own, trade(s_part, 2), after=[f_other]
    )
    t_sum, s_all = call(
        ends, [(time, BF16), ((4 * rows, half), BF16)], t_own, t_got, *chips(s_sum)
    )
    s_out, f_out, token = call(
        part(space_end),
        [((9, rows, chans), F32), ((pixels, chans), BF16), ((8, LANES), F32)],
        s_all,
        swap(s_all, 1),
        f_own,
        f_other,
        clip_g,
        scratch=[pltpu.VMEM((group, rows, 2 * half), F32)],
    )
    (t_all,) = call(
        stacked, [((4 * plan.thalf, plan.tcols), BF16)], *chips(t_sum), after=[token]
    )
    (t_out,) = call(
        part(time_end),
        [((3, chans, chans), F32)],
        t_all,
        swap(t_all, 1),
        scratch=[pltpu.VMEM((chans, plan.tcols), F32)],
    )
    return f_out.reshape(frames.shape), jnp.transpose(s_out, (1, 0, 2)), t_out


def solution(mesh):
    in_specs = (
        P("clip", "seq", None, None, None),
        P("clip", "seq", None, None, None),
        P("seq", None, None),
        P(),
    )
    out_specs = (P("clip", "seq", None, None, None), P("seq", None, None), P())

    def body(frames, cotangent, w_space, w_time):
        one, count, height, width, chans = frames.shape
        plan = Plan(mesh.shape["clip"], mesh.shape["seq"], height, width, chans)
        if one == 1 and count == 1 and plan.fits():
            return per_device(plan, frames, cotangent, w_space, w_time)
        return per_device_general(frames, cotangent, w_space, w_time)

    return jax.shard_map(body, mesh=mesh, in_specs=in_specs, out_specs=out_specs, check_vma=False)
```

```python
import functools
import math

import jax
import jax.numpy as jnp
from jax import lax
from jax.experimental import pallas as pl
from jax.experimental.pallas import tpu as pltpu
from jax.sharding import PartitionSpec as P


def padded_2(cells, sides, width):
    for axis, dim in sides:
        count = lax.axis_size(axis)
        ends = count - 1
        head = lax.slice_in_dim(cells, 0, width, axis=dim)
        tail = lax.slice_in_dim(cells, cells.shape[dim] - width, cells.shape[dim], axis=dim)
        cells = jnp.concatenate(
            [
                lax.ppermute(tail, axis, [(i, (i + 1) % count) for i in range(ends)]),
                cells,
                lax.ppermute(head, axis, [((i + 1) % count, i) for i in range(ends)]),
            ],
            axis=dim,
        )
    return cells


def temporal_grads(acts, g_pad, w_time):
    count = acts.shape[0]
    chans = acts.shape[-1]
    flat_acts = acts.reshape(-1, chans)
    act_grad = jnp.zeros(flat_acts.shape, jnp.float32)
    time_terms = []
    for k in range(3):
        shifted = g_pad[2 - k : 2 - k + count].reshape(-1, chans)
        act_grad = act_grad + lax.dot_general(
            shifted, w_time[k], (((1,), (1,)), ((), ())), preferred_element_type=jnp.float32
        )
        time_terms.append(
            lax.dot_general(
                flat_acts, shifted, (((0,), (0,)), ((), ())), preferred_element_type=jnp.float32
            )
        )
    return (act_grad.astype(jnp.bfloat16).reshape(acts.shape), jnp.stack(time_terms, axis=0))


def per_device_general(frames, cotangent, w_space, w_time):
    weights = lax.all_gather(w_space, "seq", axis=0, tiled=True)
    clip_x = frames[0]
    clip_g = cotangent[0]
    count, height, width, chans = clip_x.shape
    factor = 1.0 / math.sqrt(lax.axis_size("clip") * count * lax.axis_size("seq") * height * width)
    padded = jnp.pad(clip_x, ((0, 0), (1, 1), (1, 1), (0, 0)))
    pieces = [
        padded[:, i : i + height, j : j + width, :].reshape(-1, chans)
        for i in range(3)
        for j in range(3)
    ]
    pre_act = jnp.zeros((count * height * width, chans), jnp.float32)
    for tap in range(9):
        pre_act = pre_act + jnp.dot(
            pieces[tap], weights[:, tap, :], preferred_element_type=jnp.float32
        )
    acts = jax.nn.silu(pre_act).astype(jnp.bfloat16).reshape(1, count, height, width, chans)
    g_rims = padded_2(cotangent, (("seq", 1),), 1)
    g_pad = g_rims[0].reshape(count + 2, height * width, chans)
    act_grad, time_terms = temporal_grads(
        acts[0].reshape(count, height * width, chans), g_pad, w_time
    )
    sigma = jax.nn.sigmoid(pre_act)
    pre_grad = (
        act_grad.reshape(-1, chans).astype(jnp.float32) * sigma * (1.0 + pre_act * (1.0 - sigma))
    ).astype(jnp.bfloat16)
    terms = []
    for tap in range(9):
        part = pieces[tap]
        terms.append(
            lax.dot_general(
                part, pre_grad, (((0,), (0,)), ((), ())), preferred_element_type=jnp.float32
            )
        )
    space_share = lax.psum_scatter(
        jnp.stack(terms, axis=1) * factor, "seq", scatter_dimension=0, tiled=True
    )
    space_grad = lax.psum(space_share, "clip")
    time_grad = lax.psum(time_terms * factor, ("clip", "seq"))
    grad_pad = jnp.pad(
        pre_grad.reshape(count, height, width, chans), ((0, 0), (1, 1), (1, 1), (0, 0))
    )
    input_grad = clip_g.reshape(-1, chans).astype(jnp.float32)
    for i in range(3):
        for j in range(3):
            piece = grad_pad[:, 2 - i : 2 - i + height, 2 - j : 2 - j + width, :].reshape(-1, chans)
            input_grad = input_grad + lax.dot_general(
                piece,
                weights[:, 3 * i + j, :],
                (((1,), (1,)), ((), ())),
                preferred_element_type=jnp.float32,
            )
    frames_grad = input_grad.astype(jnp.bfloat16).reshape(1, count, height, width, chans)
    return (frames_grad, space_grad, time_grad)


BF16 = jnp.bfloat16
F32 = jnp.float32
LANES = 128
VMEM = pl.BlockSpec(memory_space=pltpu.VMEM)
NN = (((1,), (0,)), ((), ()))
NT = (((1,), (1,)), ((), ()))
TN = (((0,), (0,)), ((), ()))


def round_up(value, unit):
    return -(-value // unit) * unit


def mm(lhs, rhs, dims):
    return lax.dot_general(lhs, rhs, dims, preferred_element_type=F32)


def call(kernel, outs, *args, after=(), scratch=()):
    def body(*refs):
        kernel(*refs[: len(args)], *refs[len(args) + len(after) :])

    return pl.pallas_call(
        body,
        out_shape=tuple(jax.ShapeDtypeStruct(shape, dtype) for shape, dtype in outs),
        in_specs=[VMEM] * len(args) + [pl.BlockSpec(memory_space=pl.ANY)] * len(after),
        out_specs=(VMEM,) * len(outs),
        scratch_shapes=list(scratch),
        compiler_params=pltpu.CompilerParams(vmem_limit_bytes=48 * 1024 * 1024),
    )(*args, *after)


class Plan:
    def __init__(self, clips, seqs, height, width, chans):
        self.clips, self.seqs = clips, seqs
        self.height, self.width, self.chans = height, width, chans
        self.group = clips // 2
        self.slab = chans // max(self.group, 1)
        self.rows = chans // seqs
        self.pixels = height * width
        self.cols = 9 * self.slab
        self.half = round_up(round_up(self.cols, 2 * LANES) // 2, LANES)
        self.tcols = round_up(3 * self.slab, LANES)
        self.thalf = chans // 2
        self.chips = (0, self.group + 2, self.group, 2)
        self.factor = 1.0 / math.sqrt(clips * seqs * self.pixels)

    def fits(self):
        return (
            self.group == 4
            and self.slab * self.group == self.chans
            and self.rows * self.seqs == self.chans
            and self.slab % 16 == 0
            and self.rows % 16 == 0
            and self.thalf % 16 == 0
            and self.pixels % LANES == 0
            and self.seqs == 4
        )

    def place(self):
        clip = lax.axis_index("clip")
        return clip % self.group, clip // self.group, lax.axis_index("seq")


def prepare(plan, f_hbm, g_hbm, w_hbm, ft_ref, gt_ref, wp_ref, wh_ref, f_ref, g_ref, w_ref, sems):
    low, high, _ = plan.place()
    slab, half = plan.slab, plan.half
    copies = [
        pltpu.make_async_copy(src, dst, sems.at[index])
        for index, (src, dst) in enumerate(((g_hbm, g_ref), (w_hbm, w_ref), (f_hbm, f_ref)))
    ]
    for copy in copies:
        copy.start()
    copies[0].wait()
    gt_ref[...] = g_ref[...].T
    copies[1].wait()
    for index in range(plan.group):

        @pl.when(low == index)
        def _():
            taps = [w_ref[tap][:, slab * index : slab * (index + 1)] for tap in range(9)]
            if plan.cols < 2 * half:
                taps.append(jnp.zeros((plan.rows, 2 * half - plan.cols), BF16))
            wp_ref[...] = jnp.concatenate(taps, axis=1)

    wh_ref[...] = wp_ref[:, pl.ds(pl.multiple_of(high * half, LANES), half)]
    copies[2].wait()
    ft_ref[...] = f_ref[...].T


def shifts(plan, lanes):
    lane = lax.broadcasted_iota(jnp.int32, (1, lanes), 1) % plan.pixels
    row, col = lane // plan.width, lane % plan.width
    found = []
    for i in range(3):
        for j in range(3):
            inside = (
                (row + (i - 1) >= 0)
                & (row + (i - 1) < plan.height)
                & (col + (j - 1) >= 0)
                & (col + (j - 1) < plan.width)
            )
            found.append(((i - 1) * plan.width + (j - 1), inside))
    return found


def rolled(value, distance):
    lanes = value.shape[1]
    return value if distance == 0 else pltpu.roll(value, (-distance) % lanes, 1)


def weights(plan, *refs):
    own_ref, got_refs, other_ref = refs[0], refs[1 : plan.seqs], refs[plan.seqs]
    w_all, w_turned = refs[plan.seqs + 1 :]
    _, high, z = plan.place()
    rows, half = plan.rows, plan.half
    here = pl.ds(pl.multiple_of(high * half, LANES), half)
    there = pl.ds(pl.multiple_of((1 - high) * half, LANES), half)
    w_all[pl.ds(pl.multiple_of(z * rows, 16), rows), :] = own_ref[...]
    for k, got_ref in enumerate(got_refs, 1):
        place = pl.ds(pl.multiple_of((z - k + plan.seqs) % plan.seqs * rows, 16), rows)
        w_all[place, here] = got_ref[...]
        w_all[place, there] = other_ref[(k - 1) * rows : k * rows, :]
    w_turned[...] = w_all[...].T


def forward(plan, w_turned, *refs):
    slab = plan.slab
    frames, (f_all, a_ref, d_ref, taps) = refs[: plan.group], refs[plan.group :]
    for d, frame in enumerate(frames):
        f_all[:, d * plan.pixels : (d + 1) * plan.pixels] = frame[...]
    taps[...] = mm(w_turned[: plan.cols, :], f_all[...], NN)
    total = None
    for tap, (distance, inside) in enumerate(shifts(plan, f_all.shape[1])):
        term = rolled(taps[tap * slab : (tap + 1) * slab, :], distance)
        term = jnp.where(inside, term, 0.0)
        total = term if total is None else total + term
    sigma = 1.0 / (1.0 + jnp.exp(-total))
    a_ref[...] = (total * sigma).astype(BF16)
    d_ref[...] = sigma * (1.0 + total * (1.0 - sigma))


def act_grads(plan, before_ref, own_ref, after_ref, wt_ref, send_ref, mine_ref, core_ref, total):
    low, _, _ = plan.place()
    slab = plan.slab
    here = mm(wt_ref[0], after_ref[...], NN)
    here = here + mm(wt_ref[1], own_ref[...], NN)
    here = here + mm(wt_ref[2], before_ref[...], NN)
    total[...] = here.astype(BF16)
    for d, ref in enumerate((mine_ref, core_ref)):
        place = slice(d * slab, (d + 1) * slab)
        ref[...] = total[pl.ds(pl.multiple_of((low ^ d) * slab, 16), slab), :]
        send_ref[place, :] = total[pl.ds(pl.multiple_of((low ^ (d + 2)) * slab, 16), slab), :]


def temporal(plan, a_ref, *refs):
    group, pixels, chans = plan.group, plan.pixels, plan.chans
    here_refs, halo_refs = refs[:group], refs[group : 2 * group]
    send_ref, keep_ref, total = refs[2 * group :]
    _, high, _ = plan.place()
    acts = a_ref[...]
    after = [ref[chans:, :] for ref in halo_refs]
    before = [ref[:chans, :] for ref in halo_refs]
    parts = []
    for grads in (after, [ref[...] for ref in here_refs], before):
        term = None
        for d in range(group):
            here = mm(grads[d], acts[:, d * pixels : (d + 1) * pixels], NT)
            term = here if term is None else term + here
        parts.append(term)
    if plan.tcols > 3 * plan.slab:
        parts.append(jnp.zeros((chans, plan.tcols - 3 * plan.slab), F32))
    total[...] = jnp.concatenate(parts, axis=1)
    size = plan.thalf
    keep_ref[...] = total[pl.ds(pl.multiple_of(high * size, 16), size), :]
    send_ref[...] = total[pl.ds(pl.multiple_of((1 - high) * size, 16), size), :].astype(BF16)


def spatial(plan, w_all, f_all, d_ref, mine_ref, core_ref, pair_ref, last_ref, *refs):
    s_send, s_keep, f_send, f_keep, expanded, total = refs
    _, high, _ = plan.place()
    pixels, slab, chans = plan.pixels, plan.slab, plan.chans
    parts = [mine_ref[...], core_ref[...], pair_ref[:slab, :], last_ref[...]]
    parts = [part.astype(F32) for part in parts]
    act_grad = jnp.concatenate(parts, axis=1)
    pre_grad = (act_grad * d_ref[...]).astype(BF16).astype(F32)
    moves = shifts(plan, pre_grad.shape[1])
    for tap, (distance, _) in enumerate(moves):
        inside = moves[8 - tap][1]
        term = jnp.where(inside, rolled(pre_grad, -distance), 0.0)
        expanded[tap * slab : (tap + 1) * slab, :] = term.astype(BF16)
    total[:, : plan.cols] = mm(f_all[...], expanded[...], NT)
    if plan.cols < total.shape[1]:
        total[:, plan.cols :] = jnp.zeros((chans, total.shape[1] - plan.cols), F32)
    size = plan.half
    s_keep[...] = total[:, pl.ds(pl.multiple_of(high * size, LANES), size)]
    s_send[...] = total[:, pl.ds(pl.multiple_of((1 - high) * size, LANES), size)].astype(BF16)
    grads = mm(w_all[:, : plan.cols], expanded[...], NN)
    for index in range(2):
        d = 2 * index
        here = slice(index * chans, (index + 1) * chans)
        f_keep[here, :] = grads[:, d * pixels : (d + 1) * pixels]
        f_send[here, :] = grads[:, (d + 1) * pixels : (d + 2) * pixels].astype(BF16)


def added(keep_ref, got_ref, own_ref, send_ref):
    total = keep_ref[...] + got_ref[...].astype(F32)
    own_ref[...] = total
    send_ref[...] = total.astype(BF16)


def space_halves(plan, keep_ref, got_ref, own_ref, send_ref, total):
    _, _, z = plan.place()
    rows = plan.rows
    total[...] = keep_ref[...] + got_ref[...].astype(F32)
    for n in range(2):
        place = slice(n * rows, (n + 1) * rows)
        own_ref[place, :] = total[pl.ds(pl.multiple_of((z ^ (2 * n)) * rows, 16), rows), :]
        send_ref[place, :] = total[pl.ds(pl.multiple_of((z ^ (2 * n + 1)) * rows, 16), rows), :].astype(BF16)


def space_quarter(plan, keep_ref, got_ref, own_ref, send_ref):
    rows = plan.rows
    own_ref[...] = keep_ref[:rows, :] + got_ref[:rows, :].astype(F32)
    send_ref[...] = (keep_ref[rows:, :] + got_ref[rows:, :].astype(F32)).astype(BF16)


def summed(own_ref, *refs):
    total = own_ref[...]
    for ref in refs[:-1]:
        total = total + ref[...].astype(F32)
    refs[-1][...] = total.astype(BF16)


def stacked(*refs):
    out_ref, first = refs[-1], 0
    for ref in refs[:-1]:
        out_ref[first : first + ref.shape[0], :] = ref[...]
        first += ref.shape[0]


def frame_half(plan, keep_ref, got_ref, send_ref, own_ref):
    chans = plan.chans
    own_ref[...] = keep_ref[:chans, :] + got_ref[:chans, :].astype(F32)
    send_ref[...] = (keep_ref[chans:, :] + got_ref[chans:, :].astype(F32)).astype(BF16)


def ends(t_own, t_got, *refs):
    chips, (t_sum, s_all) = refs[:4], refs[4:]
    summed(t_own, t_got, t_sum)
    stacked(*chips, s_all)


def space_end(plan, here_ref, core_ref, f_own, f_got, g_ref, out_ref, f_out, token_ref, held):
    low, high, _ = plan.place()
    group, slab, rows = plan.group, plan.slab, plan.rows
    for core, ref in enumerate((here_ref, core_ref)):
        for chip, distance in enumerate(plan.chips):
            other = high if distance < group else 1 - high
            lane = pl.multiple_of(other * plan.half, LANES)
            piece = ref[chip * rows : (chip + 1) * rows, :].astype(F32) * plan.factor
            held[low ^ (distance % group + core), :, pl.ds(lane, plan.half)] = piece
    for tap in range(9):
        out_ref[tap] = jnp.concatenate(
            [held[index, :, tap * slab : (tap + 1) * slab] for index in range(group)], axis=1
        )
    frame = f_own[...] + f_got[...].astype(F32)
    f_out[...] = (g_ref[...].astype(F32) + frame.T).astype(BF16)
    token_ref[...] = jnp.zeros_like(token_ref)


def time_turn(plan, ref, out_ref, held):
    _, high, _ = plan.place()
    size = plan.thalf
    near = pl.ds(pl.multiple_of(high * size, 16), size)
    far = pl.ds(pl.multiple_of((1 - high) * size, 16), size)
    for pair in range(2):
        first = plan.chips.index(2 * pair) * size
        second = plan.chips.index(plan.group + 2 * pair) * size
        held[near, :] = ref[first : first + size, :].astype(F32)
        held[far, :] = ref[second : second + size, :].astype(F32)
        out_ref[pair] = held[...].T * plan.factor


def time_end(plan, here_ref, core_ref, out_ref, held, turned):
    low, _, _ = plan.place()
    slab = plan.slab
    time_turn(plan, core_ref, turned, held)
    for core, ref in enumerate((here_ref, turned)):
        for pair in range(2):
            for k in range(3):
                here = pl.ds(pl.multiple_of((low ^ (2 * pair + core)) * slab, 16), slab)
                out_ref[k, here, :] = ref[pair, k * slab : (k + 1) * slab, :]


def per_device(plan, frames, cotangent, w_space, w_time):
    pixels, chans, group, seqs = plan.pixels, plan.chans, plan.group, plan.seqs
    slab, rows, half = plan.slab, plan.rows, plan.half
    lanes = group * pixels
    part = lambda fn: functools.partial(fn, plan)

    def swap(value, distance):
        return lax.ppermute(value, "clip", [(i, i ^ distance) for i in range(plan.clips)])

    def trade(value, distance):
        return lax.ppermute(value, "seq", [(i, i ^ distance) for i in range(seqs)])

    def turn(value, k):
        return lax.ppermute(value, "seq", [(i, (i + k) % seqs) for i in range(seqs)])

    def neighbours(value):
        z = lax.axis_index("seq")
        found = []
        for first in range(2):
            other = {i: i for i in range(seqs)}
            for i in range(first, seqs - 1, 2):
                other[i], other[i + 1] = i + 1, i
            found.append(lax.ppermute(value, "seq", list(other.items())))
        low, high = jnp.where(z % 2 == 1, *found), jnp.where(z % 2 == 1, *found[::-1])
        zero = jnp.zeros_like(value)
        return jnp.where(z == 0, zero, low), jnp.where(z == seqs - 1, zero, high)

    def gathered(own, pair):
        return own, swap(own, 1), pair, swap(pair, 1)

    def chips(value):
        return (value, *(swap(value, distance) for distance in plan.chips[1:]))

    clip_f, clip_g = frames.reshape(pixels, chans), cotangent.reshape(pixels, chans)
    taps = jnp.transpose(w_space, (1, 0, 2))
    frame = (chans, pixels)
    outs = [(frame, BF16), (frame, BF16), ((rows, 2 * half), BF16), ((rows, half), BF16)]
    frame_f, frame_g, piece, half_piece = pl.pallas_call(
        part(prepare),
        out_shape=tuple(jax.ShapeDtypeStruct(shape, dtype) for shape, dtype in outs),
        in_specs=[pl.BlockSpec(memory_space=pl.ANY)] * 3,
        out_specs=(VMEM,) * len(outs),
        scratch_shapes=[
            pltpu.VMEM(clip_f.shape, BF16),
            pltpu.VMEM(clip_g.shape, BF16),
            pltpu.VMEM(taps.shape, BF16),
            pltpu.SemaphoreType.DMA((3,)),
        ],
        compiler_params=pltpu.CompilerParams(vmem_limit_bytes=55_900_000),
    )(clip_f, clip_g, taps)

    w_got = [turn(half_piece, k) for k in range(1, seqs)]
    w_other = swap(jnp.concatenate(w_got, axis=0), group)
    pair_f, pair_g = swap(frame_f, 2), swap(frame_g, 2)
    before, after = neighbours(frame_g)
    d_send, d_mine, d_core = call(
        part(act_grads),
        [((2 * slab, pixels), BF16), ((slab, pixels), BF16), ((slab, pixels), BF16)],
        before,
        frame_g,
        after,
        w_time,
        scratch=[pltpu.VMEM(frame, BF16)],
    )
    d_pair = swap(d_send, 2)
    w_all, w_turned = call(
        part(weights),
        [((chans, 2 * half), BF16), ((2 * half, chans), BF16)],
        piece,
        *w_got,
        w_other,
        after=[pair_g],
    )
    f_all, acts, slope = call(
        part(forward),
        [((chans, lanes), BF16), ((slab, lanes), BF16), ((slab, lanes), F32)],
        w_turned,
        *gathered(frame_f, pair_f),
        scratch=[pltpu.VMEM((plan.cols, lanes), F32)],
    )
    d_core, d_last = swap(d_core, 1), swap(d_pair[slab:], 1)
    (halo,) = call(
        stacked,
        [((2 * chans, pixels), BF16)],
        before,
        after,
        after=[w_all, d_pair, d_core, f_all],
    )
    s_send, s_keep, f_send, f_keep = call(
        part(spatial),
        [
            ((chans, half), BF16),
            ((chans, half), F32),
            ((2 * chans, pixels), BF16),
            ((2 * chans, pixels), F32),
        ],
        w_all,
        f_all,
        slope,
        d_mine,
        d_core,
        d_pair,
        d_last,
        scratch=[pltpu.VMEM((plan.cols, lanes), BF16), pltpu.VMEM((chans, 2 * half), F32)],
    )
    time = (plan.thalf, plan.tcols)
    t_send, t_keep = call(
        part(temporal),
        [(time, BF16), (time, F32)],
        acts,
        *gathered(frame_g, pair_g),
        *gathered(halo, swap(halo, 2)),
        scratch=[pltpu.VMEM((chans, plan.tcols), F32)],
    )

    f_half, f_own = call(
        part(frame_half), [(frame, BF16), (frame, F32)], f_keep, swap(f_send, 1)
    )
    f_other = swap(f_half, 2)
    s_own, s_part = call(
        part(space_halves),
        [((2 * rows, half), F32), ((2 * rows, half), BF16)],
        s_keep,
        swap(s_send, group),
        scratch=[pltpu.VMEM((chans, half), F32)],
    )
    s_own, s_part = call(
        part(space_quarter),
        [((rows, half), F32), ((rows, half), BF16)],
        s_own,
        trade(s_part, 1),
    )
    t_own, t_part = call(
        added, [(time, F32), (time, BF16)], t_keep, swap(t_send, group), after=[s_own]
    )
    t_own, t_part = call(added, [(time, F32), (time, BF16)], t_own, trade(t_part, 1))
    t_got = trade(t_part, 2)
    (s_sum,) = call(
        summed, [((rows, half), BF16)], s_own, trade(s_part, 2), after=[f_other]
    )
    t_sum, s_all = call(
        ends, [(time, BF16), ((4 * rows, half), BF16)], t_own, t_got, *chips(s_sum)
    )
    s_out, f_out, token = call(
        part(space_end),
        [((9, rows, chans), F32), ((pixels, chans), BF16), ((8, LANES), F32)],
        s_all,
        swap(s_all, 1),
        f_own,
        f_other,
        clip_g,
        scratch=[pltpu.VMEM((group, rows, 2 * half), F32)],
    )
    (t_all,) = call(
        stacked, [((4 * plan.thalf, plan.tcols), BF16)], *chips(t_sum), after=[token]
    )
    turned = (2, plan.tcols, chans)
    held = pltpu.VMEM((chans, plan.tcols), F32)
    (t_here,) = call(part(time_turn), [(turned, F32)], t_all, scratch=[held])
    (t_out,) = call(
        part(time_end),
        [((3, chans, chans), F32)],
        t_here,
        swap(t_all, 1),
        scratch=[held, pltpu.VMEM(turned, F32)],
    )
    return f_out.reshape(frames.shape), jnp.transpose(s_out, (1, 0, 2)), t_out


def solution(mesh):
    in_specs = (
        P("clip", "seq", None, None, None),
        P("clip", "seq", None, None, None),
        P("seq", None, None),
        P(),
    )
    out_specs = (P("clip", "seq", None, None, None), P("seq", None, None), P())

    def body(frames, cotangent, w_space, w_time):
        one, count, height, width, chans = frames.shape
        plan = Plan(mesh.shape["clip"], mesh.shape["seq"], height, width, chans)
        if one == 1 and count == 1 and plan.fits():
            return per_device(plan, frames, cotangent, w_space, w_time)
        return per_device_general(frames, cotangent, w_space, w_time)

    return jax.shard_map(body, mesh=mesh, in_specs=in_specs, out_specs=out_specs, check_vma=False)
```

```python
import functools
import math

import jax
import jax.numpy as jnp
from jax import lax
from jax.experimental import pallas as pl
from jax.experimental.pallas import tpu as pltpu
from jax.sharding import PartitionSpec as P


def padded_2(cells, sides, width):
    for axis, dim in sides:
        count = lax.axis_size(axis)
        ends = count - 1
        head = lax.slice_in_dim(cells, 0, width, axis=dim)
        tail = lax.slice_in_dim(cells, cells.shape[dim] - width, cells.shape[dim], axis=dim)
        cells = jnp.concatenate(
            [
                lax.ppermute(tail, axis, [(i, (i + 1) % count) for i in range(ends)]),
                cells,
                lax.ppermute(head, axis, [((i + 1) % count, i) for i in range(ends)]),
            ],
            axis=dim,
        )
    return cells


def temporal_grads(acts, g_pad, w_time):
    count = acts.shape[0]
    chans = acts.shape[-1]
    flat_acts = acts.reshape(-1, chans)
    act_grad = jnp.zeros(flat_acts.shape, jnp.float32)
    time_terms = []
    for k in range(3):
        shifted = g_pad[2 - k : 2 - k + count].reshape(-1, chans)
        act_grad = act_grad + lax.dot_general(
            shifted, w_time[k], (((1,), (1,)), ((), ())), preferred_element_type=jnp.float32
        )
        time_terms.append(
            lax.dot_general(
                flat_acts, shifted, (((0,), (0,)), ((), ())), preferred_element_type=jnp.float32
            )
        )
    return (act_grad.astype(jnp.bfloat16).reshape(acts.shape), jnp.stack(time_terms, axis=0))


def per_device_general(frames, cotangent, w_space, w_time):
    weights = lax.all_gather(w_space, "seq", axis=0, tiled=True)
    clip_x = frames[0]
    clip_g = cotangent[0]
    count, height, width, chans = clip_x.shape
    factor = 1.0 / math.sqrt(lax.axis_size("clip") * count * lax.axis_size("seq") * height * width)
    padded = jnp.pad(clip_x, ((0, 0), (1, 1), (1, 1), (0, 0)))
    pieces = [
        padded[:, i : i + height, j : j + width, :].reshape(-1, chans)
        for i in range(3)
        for j in range(3)
    ]
    pre_act = jnp.zeros((count * height * width, chans), jnp.float32)
    for tap in range(9):
        pre_act = pre_act + jnp.dot(
            pieces[tap], weights[:, tap, :], preferred_element_type=jnp.float32
        )
    acts = jax.nn.silu(pre_act).astype(jnp.bfloat16).reshape(1, count, height, width, chans)
    g_rims = padded_2(cotangent, (("seq", 1),), 1)
    g_pad = g_rims[0].reshape(count + 2, height * width, chans)
    act_grad, time_terms = temporal_grads(
        acts[0].reshape(count, height * width, chans), g_pad, w_time
    )
    sigma = jax.nn.sigmoid(pre_act)
    pre_grad = (
        act_grad.reshape(-1, chans).astype(jnp.float32) * sigma * (1.0 + pre_act * (1.0 - sigma))
    ).astype(jnp.bfloat16)
    terms = []
    for tap in range(9):
        part = pieces[tap]
        terms.append(
            lax.dot_general(
                part, pre_grad, (((0,), (0,)), ((), ())), preferred_element_type=jnp.float32
            )
        )
    space_share = lax.psum_scatter(
        jnp.stack(terms, axis=1) * factor, "seq", scatter_dimension=0, tiled=True
    )
    space_grad = lax.psum(space_share, "clip")
    time_grad = lax.psum(time_terms * factor, ("clip", "seq"))
    grad_pad = jnp.pad(
        pre_grad.reshape(count, height, width, chans), ((0, 0), (1, 1), (1, 1), (0, 0))
    )
    input_grad = clip_g.reshape(-1, chans).astype(jnp.float32)
    for i in range(3):
        for j in range(3):
            piece = grad_pad[:, 2 - i : 2 - i + height, 2 - j : 2 - j + width, :].reshape(-1, chans)
            input_grad = input_grad + lax.dot_general(
                piece,
                weights[:, 3 * i + j, :],
                (((1,), (1,)), ((), ())),
                preferred_element_type=jnp.float32,
            )
    frames_grad = input_grad.astype(jnp.bfloat16).reshape(1, count, height, width, chans)
    return (frames_grad, space_grad, time_grad)


BF16 = jnp.bfloat16
F32 = jnp.float32
LANES = 128
VMEM = pl.BlockSpec(memory_space=pltpu.VMEM)
NN = (((1,), (0,)), ((), ()))
NT = (((1,), (1,)), ((), ()))
TN = (((0,), (0,)), ((), ()))


def round_up(value, unit):
    return -(-value // unit) * unit


def mm(lhs, rhs, dims):
    return lax.dot_general(lhs, rhs, dims, preferred_element_type=F32)


def call(kernel, outs, *args, after=(), scratch=()):
    def body(*refs):
        kernel(*refs[: len(args)], *refs[len(args) + len(after) :])

    return pl.pallas_call(
        body,
        out_shape=tuple(jax.ShapeDtypeStruct(shape, dtype) for shape, dtype in outs),
        in_specs=[VMEM] * len(args) + [pl.BlockSpec(memory_space=pl.ANY)] * len(after),
        out_specs=(VMEM,) * len(outs),
        scratch_shapes=list(scratch),
        compiler_params=pltpu.CompilerParams(vmem_limit_bytes=48 * 1024 * 1024),
    )(*args, *after)


class Plan:
    def __init__(self, clips, seqs, height, width, chans):
        self.clips, self.seqs = clips, seqs
        self.height, self.width, self.chans = height, width, chans
        self.group = clips // 2
        self.slab = chans // max(self.group, 1)
        self.rows = chans // seqs
        self.pixels = height * width
        self.cols = 9 * self.slab
        self.half = round_up(round_up(self.cols, 2 * LANES) // 2, LANES)
        self.tcols = round_up(3 * self.slab, LANES)
        self.thalf = chans // 2
        self.chips = (0, self.group + 2, self.group, 2)
        self.factor = 1.0 / math.sqrt(clips * seqs * self.pixels)

    def fits(self):
        return (
            self.group == 4
            and self.slab * self.group == self.chans
            and self.rows * self.seqs == self.chans
            and self.slab % 16 == 0
            and self.rows % 16 == 0
            and self.thalf % 16 == 0
            and self.pixels % LANES == 0
            and self.seqs == 4
        )

    def place(self):
        clip = lax.axis_index("clip")
        return clip % self.group, clip // self.group, lax.axis_index("seq")


def prepare(plan, f_hbm, g_hbm, w_hbm, ft_ref, gt_ref, wp_ref, wh_ref, f_ref, g_ref, w_ref, sems):
    low, high, _ = plan.place()
    slab, half = plan.slab, plan.half
    copies = [
        pltpu.make_async_copy(src, dst, sems.at[index])
        for index, (src, dst) in enumerate(((g_hbm, g_ref), (w_hbm, w_ref), (f_hbm, f_ref)))
    ]
    for copy in copies:
        copy.start()
    copies[0].wait()
    gt_ref[...] = g_ref[...].T
    copies[1].wait()
    for index in range(plan.group):

        @pl.when(low == index)
        def _():
            taps = [w_ref[tap][:, slab * index : slab * (index + 1)] for tap in range(9)]
            if plan.cols < 2 * half:
                taps.append(jnp.zeros((plan.rows, 2 * half - plan.cols), BF16))
            wp_ref[...] = jnp.concatenate(taps, axis=1)

    wh_ref[...] = wp_ref[:, pl.ds(pl.multiple_of(high * half, LANES), half)]
    copies[2].wait()
    ft_ref[...] = f_ref[...].T


def shifts(plan, lanes):
    lane = lax.broadcasted_iota(jnp.int32, (1, lanes), 1) % plan.pixels
    row, col = lane // plan.width, lane % plan.width
    found = []
    for i in range(3):
        for j in range(3):
            inside = (
                (row + (i - 1) >= 0)
                & (row + (i - 1) < plan.height)
                & (col + (j - 1) >= 0)
                & (col + (j - 1) < plan.width)
            )
            found.append(((i - 1) * plan.width + (j - 1), inside))
    return found


def rolled(value, distance):
    lanes = value.shape[1]
    return value if distance == 0 else pltpu.roll(value, (-distance) % lanes, 1)


def weights(plan, *refs):
    own_ref, got_refs, other_ref = refs[0], refs[1 : plan.seqs], refs[plan.seqs]
    w_all, w_turned = refs[plan.seqs + 1 :]
    _, high, z = plan.place()
    rows, half = plan.rows, plan.half
    here = pl.ds(pl.multiple_of(high * half, LANES), half)
    there = pl.ds(pl.multiple_of((1 - high) * half, LANES), half)
    w_all[pl.ds(pl.multiple_of(z * rows, 16), rows), :] = own_ref[...]
    for k, got_ref in enumerate(got_refs, 1):
        place = pl.ds(pl.multiple_of((z - k + plan.seqs) % plan.seqs * rows, 16), rows)
        w_all[place, here] = got_ref[...]
        w_all[place, there] = other_ref[(k - 1) * rows : k * rows, :]
    w_turned[...] = w_all[...].T


def forward(plan, w_turned, *refs):
    slab = plan.slab
    frames, (f_all, a_ref, d_ref, taps) = refs[: plan.group], refs[plan.group :]
    for d, frame in enumerate(frames):
        f_all[:, d * plan.pixels : (d + 1) * plan.pixels] = frame[...]
    taps[...] = mm(w_turned[: plan.cols, :], f_all[...], NN)
    total = None
    for tap, (distance, inside) in enumerate(shifts(plan, f_all.shape[1])):
        term = rolled(taps[tap * slab : (tap + 1) * slab, :], distance)
        term = jnp.where(inside, term, 0.0)
        total = term if total is None else total + term
    sigma = 1.0 / (1.0 + jnp.exp(-total))
    a_ref[...] = (total * sigma).astype(BF16)
    d_ref[...] = sigma * (1.0 + total * (1.0 - sigma))


def act_grads(plan, before_ref, own_ref, after_ref, wt_ref, send_ref, mine_ref, core_ref, total):
    low, _, _ = plan.place()
    slab = plan.slab
    here = mm(wt_ref[0], after_ref[...], NN)
    here = here + mm(wt_ref[1], own_ref[...], NN)
    here = here + mm(wt_ref[2], before_ref[...], NN)
    total[...] = here.astype(BF16)
    for d, ref in enumerate((mine_ref, core_ref)):
        place = slice(d * slab, (d + 1) * slab)
        ref[...] = total[pl.ds(pl.multiple_of((low ^ d) * slab, 16), slab), :]
        send_ref[place, :] = total[pl.ds(pl.multiple_of((low ^ (d + 2)) * slab, 16), slab), :]


def temporal(plan, a_ref, *refs):
    group, pixels, chans = plan.group, plan.pixels, plan.chans
    here_refs, halo_refs = refs[:group], refs[group : 2 * group]
    send_ref, keep_ref, total = refs[2 * group :]
    _, high, _ = plan.place()
    acts = a_ref[...]
    after = [ref[chans:, :] for ref in halo_refs]
    before = [ref[:chans, :] for ref in halo_refs]
    parts = []
    for grads in (after, [ref[...] for ref in here_refs], before):
        term = None
        for d in range(group):
            here = mm(grads[d], acts[:, d * pixels : (d + 1) * pixels], NT)
            term = here if term is None else term + here
        parts.append(term)
    if plan.tcols > 3 * plan.slab:
        parts.append(jnp.zeros((chans, plan.tcols - 3 * plan.slab), F32))
    total[...] = jnp.concatenate(parts, axis=1)
    size = plan.thalf
    keep_ref[...] = total[pl.ds(pl.multiple_of(high * size, 16), size), :]
    send_ref[...] = total[pl.ds(pl.multiple_of((1 - high) * size, 16), size), :].astype(BF16)


def spatial(plan, w_all, f_all, d_ref, mine_ref, core_ref, pair_ref, last_ref, *refs):
    s_send, s_keep, f_send, f_keep, expanded, total = refs
    _, high, _ = plan.place()
    pixels, slab, chans = plan.pixels, plan.slab, plan.chans
    parts = [mine_ref[...], core_ref[...], pair_ref[:slab, :], last_ref[...]]
    parts = [part.astype(F32) for part in parts]
    act_grad = jnp.concatenate(parts, axis=1)
    pre_grad = (act_grad * d_ref[...]).astype(BF16).astype(F32)
    moves = shifts(plan, pre_grad.shape[1])
    for tap, (distance, _) in enumerate(moves):
        inside = moves[8 - tap][1]
        term = jnp.where(inside, rolled(pre_grad, -distance), 0.0)
        expanded[tap * slab : (tap + 1) * slab, :] = term.astype(BF16)
    total[:, : plan.cols] = mm(f_all[...], expanded[...], NT)
    if plan.cols < total.shape[1]:
        total[:, plan.cols :] = jnp.zeros((chans, total.shape[1] - plan.cols), F32)
    size = plan.half
    s_keep[...] = total[:, pl.ds(pl.multiple_of(high * size, LANES), size)]
    s_send[...] = total[:, pl.ds(pl.multiple_of((1 - high) * size, LANES), size)].astype(BF16)
    grads = mm(w_all[:, : plan.cols], expanded[...], NN)
    for index in range(2):
        d = 2 * index
        here = slice(index * chans, (index + 1) * chans)
        f_keep[here, :] = grads[:, d * pixels : (d + 1) * pixels]
        f_send[here, :] = grads[:, (d + 1) * pixels : (d + 2) * pixels].astype(BF16)


def added(keep_ref, got_ref, own_ref, send_ref):
    total = keep_ref[...] + got_ref[...].astype(F32)
    own_ref[...] = total
    send_ref[...] = total.astype(BF16)


def space_halves(plan, keep_ref, got_ref, own_ref, send_ref, total):
    _, _, z = plan.place()
    rows = plan.rows
    total[...] = keep_ref[...] + got_ref[...].astype(F32)
    for n in range(2):
        place = slice(n * rows, (n + 1) * rows)
        own_ref[place, :] = total[pl.ds(pl.multiple_of((z ^ (2 * n)) * rows, 16), rows), :]
        send_ref[place, :] = total[pl.ds(pl.multiple_of((z ^ (2 * n + 1)) * rows, 16), rows), :].astype(BF16)


def space_quarter(plan, keep_ref, got_ref, own_ref, send_ref):
    rows = plan.rows
    own_ref[...] = keep_ref[:rows, :] + got_ref[:rows, :].astype(F32)
    send_ref[...] = (keep_ref[rows:, :] + got_ref[rows:, :].astype(F32)).astype(BF16)


def summed(own_ref, *refs):
    total = own_ref[...]
    for ref in refs[:-1]:
        total = total + ref[...].astype(F32)
    refs[-1][...] = total.astype(BF16)


def stacked(*refs):
    out_ref, first = refs[-1], 0
    for ref in refs[:-1]:
        out_ref[first : first + ref.shape[0], :] = ref[...]
        first += ref.shape[0]


def frame_half(plan, keep_ref, got_ref, send_ref, own_ref):
    chans = plan.chans
    own_ref[...] = keep_ref[:chans, :] + got_ref[:chans, :].astype(F32)
    send_ref[...] = (keep_ref[chans:, :] + got_ref[chans:, :].astype(F32)).astype(BF16)


def ends(t_own, t_got, *refs):
    chips, (t_sum, s_all) = refs[:4], refs[4:]
    summed(t_own, t_got, t_sum)
    stacked(*chips, s_all)


def space_end(plan, here_ref, core_ref, f_own, f_got, g_ref, out_ref, f_out, token_ref, held):
    low, high, _ = plan.place()
    group, slab, rows = plan.group, plan.slab, plan.rows
    for core, ref in enumerate((here_ref, core_ref)):
        for chip, distance in enumerate(plan.chips):
            other = high if distance < group else 1 - high
            lane = pl.multiple_of(other * plan.half, LANES)
            piece = ref[chip * rows : (chip + 1) * rows, :].astype(F32) * plan.factor
            held[low ^ (distance % group + core), :, pl.ds(lane, plan.half)] = piece
    for tap in range(9):
        out_ref[tap] = jnp.concatenate(
            [held[index, :, tap * slab : (tap + 1) * slab] for index in range(group)], axis=1
        )
    frame = f_own[...] + f_got[...].astype(F32)
    f_out[...] = (g_ref[...].astype(F32) + frame.T).astype(BF16)
    token_ref[...] = jnp.zeros_like(token_ref)


def turned_part(plan, pair, ref, held):
    _, high, _ = plan.place()
    size = plan.thalf
    first = plan.chips.index(2 * pair) * size
    second = plan.chips.index(plan.group + 2 * pair) * size
    near = pl.ds(pl.multiple_of(high * size, 16), size)
    far = pl.ds(pl.multiple_of((1 - high) * size, 16), size)
    held[near, :] = ref[first : first + size, :].astype(F32)
    held[far, :] = ref[second : second + size, :].astype(F32)
    return held[...].T * plan.factor


def time_turn(plan, ref, out_ref, held):
    for pair in range(2):
        out_ref[pair] = turned_part(plan, pair, ref, held)


def time_end(plan, here_ref, core_ref, out_ref, held):
    low, _, _ = plan.place()
    slab = plan.slab
    for pair in range(2):
        for core, turned in enumerate((here_ref[pair], turned_part(plan, pair, core_ref, held))):
            for k in range(3):
                here = pl.ds(pl.multiple_of((low ^ (2 * pair + core)) * slab, 16), slab)
                out_ref[k, here, :] = turned[k * slab : (k + 1) * slab, :]


def per_device(plan, frames, cotangent, w_space, w_time):
    pixels, chans, group, seqs = plan.pixels, plan.chans, plan.group, plan.seqs
    slab, rows, half = plan.slab, plan.rows, plan.half
    lanes = group * pixels
    part = lambda fn: functools.partial(fn, plan)

    def swap(value, distance):
        return lax.ppermute(value, "clip", [(i, i ^ distance) for i in range(plan.clips)])

    def trade(value, distance):
        return lax.ppermute(value, "seq", [(i, i ^ distance) for i in range(seqs)])

    def turn(value, k):
        return lax.ppermute(value, "seq", [(i, (i + k) % seqs) for i in range(seqs)])

    def neighbours(value):
        z = lax.axis_index("seq")
        found = []
        for first in range(2):
            other = {i: i for i in range(seqs)}
            for i in range(first, seqs - 1, 2):
                other[i], other[i + 1] = i + 1, i
            found.append(lax.ppermute(value, "seq", list(other.items())))
        low, high = jnp.where(z % 2 == 1, *found), jnp.where(z % 2 == 1, *found[::-1])
        zero = jnp.zeros_like(value)
        return jnp.where(z == 0, zero, low), jnp.where(z == seqs - 1, zero, high)

    def gathered(own, pair):
        return own, swap(own, 1), pair, swap(pair, 1)

    def chips(value):
        return (value, *(swap(value, distance) for distance in plan.chips[1:]))

    clip_f, clip_g = frames.reshape(pixels, chans), cotangent.reshape(pixels, chans)
    taps = jnp.transpose(w_space, (1, 0, 2))
    frame = (chans, pixels)
    outs = [(frame, BF16), (frame, BF16), ((rows, 2 * half), BF16), ((rows, half), BF16)]
    frame_f, frame_g, piece, half_piece = pl.pallas_call(
        part(prepare),
        out_shape=tuple(jax.ShapeDtypeStruct(shape, dtype) for shape, dtype in outs),
        in_specs=[pl.BlockSpec(memory_space=pl.ANY)] * 3,
        out_specs=(VMEM,) * len(outs),
        scratch_shapes=[
            pltpu.VMEM(clip_f.shape, BF16),
            pltpu.VMEM(clip_g.shape, BF16),
            pltpu.VMEM(taps.shape, BF16),
            pltpu.SemaphoreType.DMA((3,)),
        ],
        compiler_params=pltpu.CompilerParams(vmem_limit_bytes=55_900_000),
    )(clip_f, clip_g, taps)

    w_got = [turn(half_piece, k) for k in range(1, seqs)]
    w_other = swap(jnp.concatenate(w_got, axis=0), group)
    pair_f, pair_g = swap(frame_f, 2), swap(frame_g, 2)
    before, after = neighbours(frame_g)
    d_send, d_mine, d_core = call(
        part(act_grads),
        [((2 * slab, pixels), BF16), ((slab, pixels), BF16), ((slab, pixels), BF16)],
        before,
        frame_g,
        after,
        w_time,
        scratch=[pltpu.VMEM(frame, BF16)],
    )
    d_pair = swap(d_send, 2)
    w_all, w_turned = call(
        part(weights),
        [((chans, 2 * half), BF16), ((2 * half, chans), BF16)],
        piece,
        *w_got,
        w_other,
        after=[pair_g],
    )
    f_all, acts, slope = call(
        part(forward),
        [((chans, lanes), BF16), ((slab, lanes), BF16), ((slab, lanes), F32)],
        w_turned,
        *gathered(frame_f, pair_f),
        scratch=[pltpu.VMEM((plan.cols, lanes), F32)],
    )
    d_core, d_last = swap(d_core, 1), swap(d_pair[slab:], 1)
    (halo,) = call(
        stacked,
        [((2 * chans, pixels), BF16)],
        before,
        after,
        after=[w_all, d_pair, d_core, f_all],
    )
    s_send, s_keep, f_send, f_keep = call(
        part(spatial),
        [
            ((chans, half), BF16),
            ((chans, half), F32),
            ((2 * chans, pixels), BF16),
            ((2 * chans, pixels), F32),
        ],
        w_all,
        f_all,
        slope,
        d_mine,
        d_core,
        d_pair,
        d_last,
        scratch=[pltpu.VMEM((plan.cols, lanes), BF16), pltpu.VMEM((chans, 2 * half), F32)],
    )
    time = (plan.thalf, plan.tcols)
    t_send, t_keep = call(
        part(temporal),
        [(time, BF16), (time, F32)],
        acts,
        *gathered(frame_g, pair_g),
        *gathered(halo, swap(halo, 2)),
        scratch=[pltpu.VMEM((chans, plan.tcols), F32)],
    )

    f_half, f_own = call(
        part(frame_half), [(frame, BF16), (frame, F32)], f_keep, swap(f_send, 1)
    )
    f_other = swap(f_half, 2)
    s_own, s_part = call(
        part(space_halves),
        [((2 * rows, half), F32), ((2 * rows, half), BF16)],
        s_keep,
        swap(s_send, group),
        scratch=[pltpu.VMEM((chans, half), F32)],
    )
    s_own, s_part = call(
        part(space_quarter),
        [((rows, half), F32), ((rows, half), BF16)],
        s_own,
        trade(s_part, 1),
    )
    t_own, t_part = call(
        added, [(time, F32), (time, BF16)], t_keep, swap(t_send, group), after=[s_own]
    )
    t_own, t_part = call(added, [(time, F32), (time, BF16)], t_own, trade(t_part, 1))
    t_got = trade(t_part, 2)
    (s_sum,) = call(
        summed, [((rows, half), BF16)], s_own, trade(s_part, 2), after=[f_other]
    )
    t_sum, s_all = call(
        ends, [(time, BF16), ((4 * rows, half), BF16)], t_own, t_got, *chips(s_sum)
    )
    s_out, f_out, token = call(
        part(space_end),
        [((9, rows, chans), F32), ((pixels, chans), BF16), ((8, LANES), F32)],
        s_all,
        swap(s_all, 1),
        f_own,
        f_other,
        clip_g,
        scratch=[pltpu.VMEM((group, rows, 2 * half), F32)],
    )
    (t_all,) = call(
        stacked, [((4 * plan.thalf, plan.tcols), BF16)], *chips(t_sum), after=[token]
    )
    turned = (2, plan.tcols, chans)
    held = pltpu.VMEM((chans, plan.tcols), F32)
    (t_here,) = call(part(time_turn), [(turned, F32)], t_all, scratch=[held])
    (t_out,) = call(
        part(time_end),
        [((3, chans, chans), F32)],
        t_here,
        swap(t_all, 1),
        scratch=[held],
    )
    return f_out.reshape(frames.shape), jnp.transpose(s_out, (1, 0, 2)), t_out


def solution(mesh):
    in_specs = (
        P("clip", "seq", None, None, None),
        P("clip", "seq", None, None, None),
        P("seq", None, None),
        P(),
    )
    out_specs = (P("clip", "seq", None, None, None), P("seq", None, None), P())

    def body(frames, cotangent, w_space, w_time):
        one, count, height, width, chans = frames.shape
        plan = Plan(mesh.shape["clip"], mesh.shape["seq"], height, width, chans)
        if one == 1 and count == 1 and plan.fits():
            return per_device(plan, frames, cotangent, w_space, w_time)
        return per_device_general(frames, cotangent, w_space, w_time)

    return jax.shard_map(body, mesh=mesh, in_specs=in_specs, out_specs=out_specs, check_vma=False)
```
